256 devices in a mesh: ctx: 32 (over z, y), tp: 8 (over x, core).
Axes of the slice: x: 4, y: 4, z: 8, core: 2. Of those that a mesh axis runs over, the one named last changes fastest.
Arguments:
- lin_query: bfloat16 [8192, 4096], P('ctx', 'tp'), may hold values from -6 to 6
- lin_key: bfloat16 [8192, 4096], P('ctx', 'tp'), may hold values from -0.35 to 0.35
- lin_value: bfloat16 [8192, 4096], P('ctx', 'tp'), may hold values from -7 to 7
- log_decay: float32 [32, 8192], P('tp', 'ctx'), may hold values from -1 to 0
- norm_gain: float32 [4096], P('tp'), may hold values from 0.5 to 1.5
- lin_gate: bfloat16 [8192, 4096], P('ctx', 'tp'), may hold values from -6 to 6
- lin_grad: bfloat16 [8192, 4096], P('ctx', 'tp'), may hold values from -6 to 6
- soft_query: bfloat16 [8192, 4096], P('ctx', 'tp'), may hold values from -6 to 6
- soft_key: bfloat16 [8192, 1024], P('ctx', 'tp'), may hold values from -6 to 6
- soft_value: bfloat16 [8192, 1024], P('ctx', 'tp'), may hold values from -6 to 6
- soft_grad: bfloat16 [8192, 4096], P('ctx', 'tp'), may hold values from -6 to 6
Outputs:
- lin_out: bfloat16 [8192, 4096], P('ctx', 'tp')
- lin_query_grad: bfloat16 [8192, 4096], P('ctx', 'tp')
- lin_key_grad: bfloat16 [8192, 4096], P('ctx', 'tp')
- lin_value_grad: bfloat16 [8192, 4096], P('ctx', 'tp')
- lin_gate_grad: bfloat16 [8192, 4096], P('ctx', 'tp')
- soft_out: bfloat16 [8192, 4096], P('ctx', 'tp')
- soft_query_grad: bfloat16 [8192, 4096], P('ctx', 'tp')
- soft_key_grad: bfloat16 [8192, 1024], P('ctx', 'tp')
- soft_value_grad: bfloat16 [8192, 1024], P('ctx', 'tp')
The draws below stay inside these ranges and needn't reach their ends.
All inputs are finite; a program needn't handle non-finite values.
Results may differ from the reference program's by a relative error of at most 0.035.
Values may be sent and summed in bfloat16 or wider, within the bound.
A program may use at most 128 MiB of HBM per device.

```python
import math
import jax
import jax.numpy as jnp
from jax import lax

DH = 128
LINEAR_HEADS = 32
QS = 32
KVS = 8
TOK_DEV = 256
TOKEN_COUNT = 8192
N_CTX = 32


def head_classes(key, fast_share, medium_share):
    pick = jax.random.uniform(jax.random.fold_in(key, 41), (LINEAR_HEADS,), jnp.float32, 0.0, 1.0)
    fast_heads = pick < fast_share
    medium_heads = (pick >= fast_share) & (pick < fast_share + medium_share)
    phase = jax.random.randint(jax.random.fold_in(key, 43), (LINEAR_HEADS,), 0, 8)
    return (fast_heads, medium_heads, phase)


def draw_lin_key(key, part):
    width = LINEAR_HEADS * DH
    fast_share = 0.25
    medium_share = 0.25
    base = jax.random.normal(jax.random.fold_in(key, 4), (TOKEN_COUNT, width), jnp.float32) * DH ** (-0.5)
    base = jnp.clip(base, -0.35, 0.35)
    fast_heads, medium_heads, phase = head_classes(key, fast_share, medium_share)
    block_ids = jnp.arange(TOKEN_COUNT) // TOK_DEV
    loud_blocks = (block_ids[:, None] + phase[None, :]) % 8 == 0
    head_level = jnp.where(medium_heads[None, :], jnp.where(loud_blocks, 1.0, 0.02), 0.1)
    level = jnp.repeat(head_level, DH, axis=1)
    return (base * level).astype(jnp.bfloat16)


def draw_lin_value(key, part):
    width = LINEAR_HEADS * DH
    fraction = jnp.arange(width, dtype=jnp.float32) / (width - 1)
    base = jnp.clip(jax.random.normal(jax.random.fold_in(key, 3), (TOKEN_COUNT, width), jnp.float32), -4.0, 4.0)
    column_scale = jnp.exp(fraction * 0.5 * math.log(3.0))
    return (base * column_scale[None, :]).astype(jnp.bfloat16)


def draw_log_decay(key, part):
    random_root_key = jax.random.fold_in(key, 5)
    medium_random_key, gradual_random_key, machine_random_key, spike_random_key, position_random_key, noise_random_key = jax.random.split(random_root_key, 6)
    fast_share = 0.25
    medium_share = 0.25
    fast_heads, medium_heads, phase = head_classes(key, fast_share, medium_share)
    fast_rate = jnp.exp(jax.random.uniform(noise_random_key, (LINEAR_HEADS, 1), jnp.float32, math.log(0.012), math.log(0.02)))
    medium_rate = 0.5 / TOK_DEV * jnp.exp(jax.random.uniform(medium_random_key, (LINEAR_HEADS, 1), jnp.float32, 0.0, math.log(1.4)))
    slow_rate = 0.2 / TOKEN_COUNT * jnp.exp(jax.random.uniform(gradual_random_key, (LINEAR_HEADS, 1), jnp.float32, 0.0, math.log(2.0)))
    head_decay_rate = jnp.where(fast_heads[:, None], fast_rate, jnp.where(medium_heads[:, None], medium_rate, slow_rate))
    machine_factor = jnp.exp(jax.random.uniform(machine_random_key, (LINEAR_HEADS, TOKEN_COUNT // TOK_DEV), jnp.float32, 0.0, math.log(2.0)))
    machine_factor = jnp.repeat(machine_factor, TOK_DEV, axis=1)
    places = jax.random.randint(position_random_key, (2,), 0, TOKEN_COUNT)
    struck_rows = jnp.any(jnp.arange(TOKEN_COUNT)[None, :] == places[:, None], axis=0)
    spike_depth = jnp.log(jax.random.uniform(spike_random_key, (LINEAR_HEADS, TOKEN_COUNT), jnp.float32, 0.5, 0.8))
    return -head_decay_rate * machine_factor + jnp.where(struck_rows[None, :], spike_depth, 0.0)


def draw_soft_query(key, part):
    width = QS * DH
    base = jnp.clip(2.0 * jax.random.normal(jax.random.fold_in(key, 1), (TOKEN_COUNT, width), jnp.float32), -6.0, 6.0)
    return base.astype(jnp.bfloat16)


def draw_soft_key(key, part):
    width = KVS * DH
    base = jnp.clip(jax.random.normal(jax.random.fold_in(key, 2), (TOKEN_COUNT, width), jnp.float32), -4.0, 4.0)
    loud_rows = TOKEN_COUNT - 1 - jax.random.randint(jax.random.fold_in(key, 7), (KVS,), 0, 8)
    loud_signs = jnp.where(jax.random.bernoulli(jax.random.fold_in(key, 9), 0.5, (width,)), 6.0, -6.0)
    column_head = jnp.arange(width) // DH
    column_row = jnp.sum(jnp.where(column_head[:, None] == jnp.arange(KVS)[None, :], loud_rows[None, :], 0), axis=1)
    struck = jnp.arange(TOKEN_COUNT)[:, None] == column_row[None, :]
    base = jnp.where(struck, loud_signs[None, :], base)
    return base.astype(jnp.bfloat16)


def level_of(stream_key, shape, shards, least, largest):
    gain = 1.0
    for axis_at, shards_of in shards:
        draws = jax.random.uniform(jax.random.fold_in(jax.random.fold_in(stream_key, 6), axis_at), (shards_of,), jnp.float32, least / len(shards), largest / len(shards))
        gain = gain * jnp.repeat(jnp.exp(draws), shape[axis_at] // shards_of).reshape((-1,) + (1,) * (len(shape) - 1 - axis_at))
    return gain


def noise(own_key, extent, scale, bound, cuts=(), kind=jnp.bfloat16):
    drawn = scale * jax.random.normal(own_key, extent, jnp.float32)
    if cuts:
        drawn = drawn * level_of(own_key, extent, cuts, -0.22, 0.18)
    return jnp.clip(drawn, -bound, bound).astype(kind)


def setup_inputs(seed: int = 0) -> dict:
    key_list = jax.random.split(jax.random.key(seed), 12)
    lin_query = noise(key_list[0], (TOKEN_COUNT, LINEAR_HEADS * DH), 1.0, 6.0, ((0, 32), (1, 8)))
    lin_key = draw_lin_key(jax.random.fold_in(key_list[11], 71), 0)
    lin_value = draw_lin_value(jax.random.fold_in(key_list[11], 71), 0)
    log_decay = draw_log_decay(jax.random.fold_in(key_list[11], 71), 0)
    norm_gain = jnp.clip(1.0 + 0.1 * jax.random.normal(key_list[4], (LINEAR_HEADS * DH,), jnp.float32), 0.5, 1.5)
    lin_gate = noise(key_list[5], (TOKEN_COUNT, LINEAR_HEADS * DH), 1.0, 6.0, ((0, 32), (1, 8)))
    lin_grad = noise(key_list[6], (TOKEN_COUNT, LINEAR_HEADS * DH), 1.0, 6.0, ((0, 32), (1, 8)))
    soft_query = draw_soft_query(jax.random.fold_in(key_list[11], 71), 0)
    soft_key = draw_soft_key(jax.random.fold_in(key_list[11], 71), 0)
    soft_value = noise(key_list[9], (TOKEN_COUNT, KVS * DH), 1.0, 6.0, ((0, 32), (1, 8)))
    soft_grad = noise(key_list[10], (TOKEN_COUNT, QS * DH), 1.0, 6.0, ((0, 32), (1, 8)))
    return dict(lin_query=lin_query, lin_key=lin_key, lin_value=lin_value, log_decay=log_decay, norm_gain=norm_gain, lin_gate=lin_gate, lin_grad=lin_grad, soft_query=soft_query, soft_key=soft_key, soft_value=soft_value, soft_grad=soft_grad)


top_precision = lax.Precision.HIGHEST

def round_bf16(values):
    return lax.optimization_barrier(values.astype(jnp.bfloat16)).astype(jnp.float32)

def block_parts(log_block):
    blocklog = jnp.cumsum(log_block, axis=1)
    totals = blocklog[:, -1]
    order_ids = jnp.arange(log_block.shape[1])
    causal = (order_ids[:, None] >= order_ids[None, :])[None]
    spread = blocklog[:, :, None] - blocklog[:, None, :]
    decay_mask = jnp.where(causal, jnp.exp(jnp.where(causal, spread, 0.0)), 0.0)
    tail_decay = jnp.exp(totals[:, None] - blocklog).T[:, :, None]
    lead_decay = jnp.exp(blocklog).T[:, :, None]
    return (decay_mask, tail_decay, lead_decay, totals)

def lightning_reference(lin_query, lin_key, lin_value, log_decay, norm_gain, lin_gate, lin_grad):
    width = LINEAR_HEADS * DH
    shape_four = (N_CTX, TOK_DEV, LINEAR_HEADS, DH)
    query_blocks = lin_query.reshape(shape_four)
    key_blocks = lin_key.reshape(shape_four)
    value_blocks = lin_value.reshape(shape_four)
    log_blocks = log_decay.reshape(LINEAR_HEADS, N_CTX, TOK_DEV).transpose(1, 0, 2)

    def forward_step(chain_state, block_data):
        query_block, key_block, value_block, log_block = block_data
        decay_mask, tail_decay, lead_decay, totals = block_parts(log_block)
        query_f = query_block.astype(jnp.float32)
        key_f = key_block.astype(jnp.float32)
        value_f = value_block.astype(jnp.float32)
        raw_scores = jnp.einsum('thd,shd->hts', query_f, key_f, precision=top_precision)
        weights = round_bf16(raw_scores * decay_mask)
        attended = jnp.einsum('hts,she->the', weights, value_f, precision=top_precision)
        attended = attended + jnp.einsum('thd,hde->the', query_f * lead_decay, chain_state, precision=top_precision)
        local_state = jnp.einsum('shd,she->hde', key_f * tail_decay, value_f, precision=top_precision)
        following = jnp.exp(totals)[:, None, None] * chain_state + local_state
        return (following, (attended, chain_state))
    initial = jnp.zeros((LINEAR_HEADS, DH, DH), jnp.float32)
    _, (attended, carried) = lax.scan(forward_step, initial, (query_blocks, key_blocks, value_blocks, log_blocks))
    flat_out = attended.reshape(TOKEN_COUNT, width)
    scaling = lax.rsqrt(lax.optimization_barrier(jnp.sum(flat_out * flat_out, axis=1)) / width + 1e-05)[:, None]
    normed = flat_out * scaling
    gate_sig = jax.nn.sigmoid(lin_gate.astype(jnp.float32))
    gain_row = norm_gain[None, :]
    lin_out = (normed * gain_row * gate_sig).astype(jnp.bfloat16)
    grad_f = lin_grad.astype(jnp.float32)
    scaled = grad_f * gain_row * gate_sig
    gate_grad = (grad_f * normed * gain_row * gate_sig * (1.0 - gate_sig)).astype(jnp.bfloat16)
    cross_term = lax.optimization_barrier(jnp.sum(scaled * normed, axis=1)) / width
    att_grad = scaling * (scaled - normed * cross_term[:, None])
    grad_blocks = att_grad.astype(jnp.bfloat16).reshape(shape_four)

    def backward_step(chain_grad, block_data):
        query_block, key_block, value_block, log_block, grad_block, chain_state = block_data
        decay_mask, tail_decay, lead_decay, totals = block_parts(log_block)
        query_f = query_block.astype(jnp.float32)
        key_f = key_block.astype(jnp.float32)
        value_f = value_block.astype(jnp.float32)
        grad_blk = grad_block.astype(jnp.float32)
        raw_scores = jnp.einsum('thd,shd->hts', query_f, key_f, precision=top_precision)
        weights = round_bf16(raw_scores * decay_mask)
        grad_raw = jnp.einsum('the,she->hts', grad_blk, value_f, precision=top_precision)
        grad_weights = round_bf16(grad_raw * decay_mask)
        query_grad = jnp.einsum('hts,shd->thd', grad_weights, key_f, precision=top_precision)
        query_grad = query_grad + jnp.einsum('the,hde->thd', grad_blk * lead_decay, chain_state, precision=top_precision)
        key_grad = jnp.einsum('hts,thd->shd', grad_weights, query_f, precision=top_precision)
        key_grad = key_grad + jnp.einsum('she,hde->shd', value_f * tail_decay, chain_grad, precision=top_precision)
        value_grad = jnp.einsum('hts,the->she', weights, grad_blk, precision=top_precision)
        value_grad = value_grad + jnp.einsum('shd,hde->she', key_f * tail_decay, chain_grad, precision=top_precision)
        local_grad = jnp.einsum('thd,the->hde', query_f * lead_decay, grad_blk, precision=top_precision)
        following = jnp.exp(totals)[:, None, None] * chain_grad + local_grad
        return (following, (query_grad, key_grad, value_grad))
    _, (query_grad, key_grad, value_grad) = lax.scan(backward_step, initial, (query_blocks, key_blocks, value_blocks, log_blocks, grad_blocks, carried), reverse=True)
    return (lin_out, query_grad.reshape(TOKEN_COUNT, width).astype(jnp.bfloat16), key_grad.reshape(TOKEN_COUNT, width).astype(jnp.bfloat16), value_grad.reshape(TOKEN_COUNT, width).astype(jnp.bfloat16), gate_grad)

def soft_reference(soft_query, soft_key, soft_value, soft_grad):
    group_size = QS // KVS
    score_scale = DH ** (-0.5)
    query_heads = soft_query.reshape(TOKEN_COUNT, KVS, group_size, DH).transpose(1, 0, 2, 3)
    grad_heads = soft_grad.reshape(TOKEN_COUNT, KVS, group_size, DH).transpose(1, 0, 2, 3)
    key_heads = soft_key.reshape(TOKEN_COUNT, KVS, DH).transpose(1, 0, 2)
    value_heads = soft_value.reshape(TOKEN_COUNT, KVS, DH).transpose(1, 0, 2)
    block_rows = min(512, TOKEN_COUNT)
    block_count = TOKEN_COUNT // block_rows
    key_ids = jnp.arange(TOKEN_COUNT)

    def per_head(head_data):
        query_head, grad_head, key_head, value_head = head_data
        key_f = key_head.astype(jnp.float32)
        value_f = value_head.astype(jnp.float32)

        def block_step(running, block_index):
            start_row = (block_index * block_rows).astype(jnp.int32)
            query_f = lax.dynamic_slice_in_dim(query_head, start_row, block_rows, 0).astype(jnp.float32)
            grad_f = lax.dynamic_slice_in_dim(grad_head, start_row, block_rows, 0).astype(jnp.float32)
            positions = start_row + jnp.arange(block_rows)
            allowed = (positions[:, None] >= key_ids[None, :])[None]
            scores = jnp.einsum('rgd,cd->grc', query_f, key_f, precision=top_precision) * score_scale
            row_peak = lax.optimization_barrier(jnp.max(jnp.where(allowed, scores, -jnp.inf), axis=-1))
            raw_probs = jnp.where(allowed, jnp.exp(scores - row_peak[..., None]), 0.0)
            row_total = lax.optimization_barrier(jnp.sum(raw_probs, axis=-1))
            weights = round_bf16(raw_probs)
            out_f = jnp.einsum('grc,cd->grd', weights, value_f, precision=top_precision) / row_total[..., None]
            out_block = out_f.transpose(1, 0, 2).astype(jnp.bfloat16)
            out_back = lax.optimization_barrier(out_block).astype(jnp.float32)
            logsum = row_peak + jnp.log(row_total)
            delta_rows = lax.optimization_barrier(jnp.sum(grad_f * out_back, axis=-1)).T
            probs = jnp.where(allowed, jnp.exp(scores - logsum[..., None]), 0.0)
            prob_grad = jnp.einsum('rgd,cd->grc', grad_f, value_f, precision=top_precision)
            score_grad = round_bf16(probs * (prob_grad - delta_rows[..., None]))
            query_grad = (jnp.einsum('grc,cd->rgd', score_grad, key_f, precision=top_precision) * score_scale).astype(jnp.bfloat16)
            key_acc = running[0] + jnp.einsum('grc,rgd->cd', score_grad, query_f, precision=top_precision) * score_scale
            value_acc = running[1] + jnp.einsum('grc,rgd->cd', round_bf16(probs), grad_f, precision=top_precision)
            return ((key_acc, value_acc), (out_block, query_grad))
        zero_rows = jnp.zeros((TOKEN_COUNT, DH), jnp.float32)
        (key_acc, value_acc), (outs, query_grads) = lax.scan(block_step, (zero_rows, zero_rows), jnp.arange(block_count))
        return (outs.reshape(TOKEN_COUNT, group_size, DH), query_grads.reshape(TOKEN_COUNT, group_size, DH), key_acc.astype(jnp.bfloat16), value_acc.astype(jnp.bfloat16))
    outs, query_grads, key_grads, value_grads = lax.map(per_head, (query_heads, grad_heads, key_heads, value_heads))
    soft_out = outs.transpose(1, 0, 2, 3).reshape(TOKEN_COUNT, QS * DH)
    query_grad = query_grads.transpose(1, 0, 2, 3).reshape(TOKEN_COUNT, QS * DH)
    key_grad = key_grads.transpose(1, 0, 2).reshape(TOKEN_COUNT, KVS * DH)
    value_grad = value_grads.transpose(1, 0, 2).reshape(TOKEN_COUNT, KVS * DH)
    return (soft_out, query_grad, key_grad, value_grad)

def reference(lin_query, lin_key, lin_value, log_decay, norm_gain, lin_gate, lin_grad, soft_query, soft_key, soft_value, soft_grad):
    lin_out, lin_query_grad, lin_key_grad, lin_value_grad, lin_gate_grad = lightning_reference(lin_query, lin_key, lin_value, log_decay, norm_gain, lin_gate, lin_grad)
    soft_out, soft_query_grad, soft_key_grad, soft_value_grad = soft_reference(soft_query, soft_key, soft_value, soft_grad)
    return (lin_out, lin_query_grad, lin_key_grad, lin_value_grad, lin_gate_grad, soft_out, soft_query_grad, soft_key_grad, soft_value_grad)
```

```python
import math

import jax
import jax.numpy as jnp
from jax import lax
from jax.experimental import pallas as pl
from jax.experimental.pallas import tpu as pltpu
from jax.sharding import PartitionSpec as P

DH = 128
HEADS = 4
TOK = 256
NY = 4
NZ = 8
NT = 8
ROW = NY * TOK
WIDTH = 4096
MSG = DH + 16
F32 = jnp.float32
BF16 = jnp.bfloat16
MESH = pl.DeviceIdType.MESH
SCALE = DH ** (-0.5)
LOG2E = math.log2(math.e)
EXP_SCALE = SCALE * LOG2E
NEG = -1e30
EXACT = lax.Precision.HIGHEST


def nn(a, b, precision=None):
    return lax.dot_general(a, b, (((1,), (0,)), ((), ())), precision=precision, preferred_element_type=F32)


def nt(a, b, precision=None):
    return lax.dot_general(a, b, (((1,), (1,)), ((), ())), precision=precision, preferred_element_type=F32)


def tn(a, b, precision=None):
    return lax.dot_general(a, b, (((0,), (0,)), ((), ())), precision=precision, preferred_element_type=F32)


def cols(h):
    return slice(h * DH, (h + 1) * DH)


def kernel(
    lq, lk, lv, ld, gain, gate, lgrad, sq, sk, sv, so,
    lin_out, dlq, dlk, dlv, dgate, sout, dsq, dsk, dsv,
    kall, vall, q_t, g_t, v_t, k_t, peak, total, out_t, log_s, delta_s, dq_t, dk_acc, dv_acc,
    dks, dkr, dvs, dvy, dv_own, dvz, dvr, dky,
    decay, weights, gweights, tail_s, lead_s, att, gr_att, msg, st, pre, lead_tot, rmsg, rst, cmsg, car, tps, tpr,
    ky_s, ky_r, ks_s, kr_r, vs_s, vr_r, vy_s, vy_r, p1_s, p1_r, p2_s, p2_r, p3_s, p3_r, tp_s, tp_r,
    dk_s, dk_r, dv_s, dv_r, dvy_s, dvy_r, dky_s, dky_r,
):
    ctx = lax.axis_index("ctx")
    tp = lax.axis_index("tp")
    z = lax.div(ctx, NY)
    y = lax.rem(ctx, NY)

    def at_ctx(zz, yy):
        return {"ctx": zz * NY + yy}

    def y_peer(j):
        return lax.rem(y + j, NY)

    def y_from(j):
        return lax.rem(y + NY - j, NY)

    def copy(src, dst, s, r, device):
        return pltpu.make_async_remote_copy(
            src_ref=src, dst_ref=dst, send_sem=s, recv_sem=r, device_id=device, device_id_type=MESH
        )

    neighbour = at_ctx(z, y_peer(1))

    def arrived(dst, r, s):
        copy(dst, dst, s, r, neighbour).wait_recv()

    def sent(src, s, r):
        copy(src, src, s, r, neighbour).wait_send()

    barrier = pltpu.get_barrier_semaphore()
    for j in range(1, NY):
        pl.semaphore_signal(barrier, inc=1, device_id=at_ctx(z, y_peer(j)), device_id_type=MESH)
    for j in range(1, NZ):
        pl.semaphore_signal(barrier, inc=1, device_id=at_ctx(lax.rem(z + j, NZ), y), device_id_type=MESH)
    for j in range(1, NT):
        pl.semaphore_signal(barrier, inc=1, device_id={"tp": lax.rem(tp + j, NT)}, device_id_type=MESH)
    pl.semaphore_wait(barrier, NY + NZ + NT - 3)

    def block_at(zz, yy):
        return pl.ds(pl.multiple_of((zz * NY + yy) * TOK, TOK), TOK)

    def row_at(zz):
        return pl.ds(pl.multiple_of(zz * ROW, ROW), ROW)

    def key_to_peer(j):
        return copy(sk, kall.at[block_at(z, y)], ky_s.at[j - 1], ky_r.at[j - 1], at_ctx(z, y_peer(j)))

    def value_to_peer(d, j):
        ref = vall.at[block_at(z - d, y)]
        at = d * 3 + j - 1
        return copy(ref, ref, vy_s.at[at], vy_r.at[at], at_ctx(z, y_peer(j)))

    def row_to(d, to_z, to_d, at):
        ref = kall.at[row_at(z - d)]
        return copy(ref, ref, ks_s.at[at], kr_r.at[to_d], at_ctx(to_z, y))

    def value_to(d, to_z, to_d, at):
        ref = vall.at[block_at(z - d, y)]
        return copy(ref, ref, vs_s.at[at], vr_r.at[to_d], at_ctx(to_z, y))

    up = z < NZ - 1
    low = z <= 2
    last = NZ - 1

    def fetch(d):
        @pl.when(z >= d)
        def _():
            arrived(vall.at[block_at(z - d, y)], vr_r.at[d], vs_s.at[d])

            @pl.when((d <= 3) & up)
            def _():
                value_to(d, z + 1, d + 1, d).start()

            @pl.when(d >= 6)
            def _():
                value_to(d, z - 1, d - 1, d).start()

            for j in range(1, NY):
                value_to_peer(d, j).start()
            arrived(kall.at[row_at(z - d)], kr_r.at[d], ks_s.at[d])

            @pl.when((d <= 3) & up)
            def _():
                row_to(d, z + 1, d + 1, d).start()

            @pl.when(d >= 6)
            def _():
                row_to(d, z - 1, d - 1, d).start()

    def peer_values(d):
        for j in range(1, NY):
            at = d * 3 + j - 1
            arrived(vall.at[block_at(z - d, y_from(j))], vy_r.at[at], vy_s.at[at])

    kall[block_at(z, y), :] = sk[...]
    vall[block_at(z, y), :] = sv[...]
    for j in range(1, NY):
        key_to_peer(j).start()

    @pl.when(up)
    def _():
        value_to(0, z + 1, 1, 0).start()

    @pl.when(low)
    def _():
        value_to(0, last, last - z, 4).start()

    for j in range(1, NY):
        value_to_peer(0, j).start()

    for h in range(HEADS):
        q_t[h] = sq[:, cols(h)].T
        g_t[h] = so[:, cols(h)].T

    for j in range(1, NY):
        arrived(kall.at[block_at(z, y_from(j))], ky_r.at[j - 1], ky_s.at[j - 1])

    @pl.when(up)
    def _():
        row_to(0, z + 1, 1, 0).start()

    @pl.when(low)
    def _():
        row_to(0, last, last - z, 4).start()

    def coded(tot):
        first = tot.astype(BF16).astype(F32)
        second = (tot - first).astype(BF16).astype(F32)
        third = (tot - first - second).astype(BF16).astype(F32)
        r = lax.broadcasted_iota(jnp.int32, (16, DH), 0)
        rows = jnp.where(r == 0, first, jnp.where(r == 1, second, jnp.where(r == 2, third, 0.0)))
        return rows.astype(BF16)

    def decoded(rows):
        return jnp.sum(rows.astype(F32), axis=0, keepdims=True)

    def state_to_peer(k, j):
        at = k * 3 + j - 1
        return copy(msg.at[k, y_peer(j)], st.at[k, y], p1_s.at[at], p1_r.at[at], at_ctx(z, y_peer(j)))

    def total_to(k, zz):
        return copy(rmsg.at[k], rst.at[k, z], p2_s.at[k * NZ + zz], p2_r.at[k * NZ + z], at_ctx(zz, y))

    def carried_to_peer(k, j):
        at = k * 3 + j - 1
        return copy(cmsg.at[k, y_peer(j)], car.at[k, y], p3_s.at[at], p3_r.at[at], at_ctx(z, y_peer(j)))

    def send_states(k):
        st[k, y] = msg[k, y]
        for j in range(1, NY):
            state_to_peer(k, j).start()

    def z_targets(k):
        return (z + 1, NZ) if k == 0 else (0, z)

    def join_row(k):
        for j in range(1, NY):
            at = k * 3 + j - 1
            arrived(st.at[k, y_from(j)], p1_r.at[at], p1_s.at[at])
        order = range(NY) if k == 0 else range(NY - 1, -1, -1)
        state = jnp.zeros((DH, DH), F32)
        so_far = jnp.zeros((1, DH), F32)
        for i in order:
            pre[i] = state
            lead_tot[i] = so_far
            tot = decoded(st[k, i, DH:, :])
            state = jnp.exp(tot) * state + st[k, i, :DH, :].astype(F32)
            so_far = so_far + tot
        rmsg[k, :DH, :] = state.astype(BF16)
        rmsg[k, DH:, :] = coded(so_far)

        def one(zz, c):
            total_to(k, zz).start()
            return c

        lax.fori_loop(*z_targets(k), one, 0)

    def join_all(k):
        def one(i, state):
            zz = i if k == 0 else NZ - 1 - i
            at = k * NZ + zz
            arrived(rst.at[k, zz], p2_r.at[at], p2_s.at[at])
            return jnp.exp(decoded(rst[k, zz, DH:, :])) * state + rst[k, zz, :DH, :].astype(F32)

        state = lax.fori_loop(0, z if k == 0 else NZ - 1 - z, one, jnp.zeros((DH, DH), F32))
        for i in range(NY):
            cmsg[k, i] = (pre[i] + jnp.exp(lead_tot[i]) * state).astype(BF16)
        car[k, y] = cmsg[k, y]
        for j in range(1, NY):
            carried_to_peer(k, j).start()

    def take_carried(k):
        for j in range(1, NY):
            at = k * 3 + j - 1
            arrived(car.at[k, y_from(j)], p3_r.at[at], p3_s.at[at])

    logs = jnp.concatenate([ld[...], jnp.zeros((8 - HEADS, TOK), F32)], axis=0)
    earlier = lax.broadcasted_iota(jnp.int32, (TOK, TOK), 0)
    later = lax.broadcasted_iota(jnp.int32, (TOK, TOK), 1)
    log_rows = nn(logs, (earlier <= later).astype(F32), EXACT)
    log_cols = nt((later <= earlier).astype(F32), logs, EXACT)
    causal = earlier >= later
    for h in range(HEADS):
        col = log_cols[:, h : h + 1]
        row = log_rows[h : h + 1, :]
        tot = log_rows[h : h + 1, TOK - 1 :]
        dec = jnp.exp(jnp.where(causal, col - row, NEG))
        decay[h] = dec
        tail = jnp.broadcast_to(jnp.exp(tot - col), (TOK, DH))
        tail_s[h] = tail
        lead_s[h] = jnp.broadcast_to(jnp.exp(col), (TOK, DH))
        kk = lk[:, cols(h)]
        weights[h] = (nt(lq[:, cols(h)], kk) * dec).astype(BF16)
        msg[0, h, :DH, :] = tn((kk.astype(F32) * tail).astype(BF16), lv[:, cols(h)]).astype(BF16)
        code = coded(jnp.broadcast_to(tot, (1, DH)))
        msg[0, h, DH:, :] = code
        msg[1, h, DH:, :] = code
    send_states(0)

    def gated(h):
        sig = jax.nn.sigmoid(gate[:, cols(h)].astype(F32))
        return sig, gain[:, cols(h)], lgrad[:, cols(h)].astype(F32)

    def sums_to(j):
        return copy(tps, tpr.at[j], tp_s.at[j - 1], tp_r.at[j - 1], {"tp": lax.rem(tp + j, NT)})

    def attend():
        take_carried(0)
        squares = jnp.zeros((TOK, DH), F32)
        cross = jnp.zeros((TOK, DH), F32)
        for h in range(HEADS):
            a = nn(weights[h], lv[:, cols(h)]) + lead_s[h] * nn(lq[:, cols(h)], car[0, h])
            att[:, cols(h)] = a
            sig, gn, gr = gated(h)
            squares = squares + a * a
            cross = cross + gr * gn * sig * a
        ones = jnp.ones((8, DH), F32)
        tps[0:8, :] = nt(ones, squares, EXACT)
        tps[8:16, :] = nt(ones, cross, EXACT)
        for j in range(1, NT):
            sums_to(j).start()

    def norm_and_grad():
        tot = tps[...]
        for j in range(1, NT):
            arrived(tpr.at[j], tp_r.at[j - 1], tp_s.at[j - 1])
            tot = tot + tpr[j]
        rms_row = lax.rsqrt(tot[0:8] / WIDTH + 1e-05)
        mean_row = rms_row * tot[8:16] / WIDTH
        eye = (earlier == later).astype(F32)
        rms = nt(eye, rms_row, EXACT)[:, 0:1]
        mean = nt(eye, mean_row, EXACT)[:, 0:1]
        for h in range(HEADS):
            sig, gn, gr = gated(h)
            normed = att[:, cols(h)] * rms
            by_gain = normed * gn * sig
            lin_out[:, cols(h)] = by_gain.astype(BF16)
            dgate[:, cols(h)] = (gr * by_gain * (1.0 - sig)).astype(BF16)
            da = (rms * (gr * gn * sig - normed * mean)).astype(BF16)
            gr_att[:, cols(h)] = da
            gweights[h] = (nt(da, lv[:, cols(h)]) * decay[h]).astype(BF16)
            msg[1, h, :DH, :] = tn((lq[:, cols(h)].astype(F32) * lead_s[h]).astype(BF16), da).astype(BF16)
        send_states(1)

    def lin_grads():
        take_carried(1)
        for h in range(HEADS):
            da = gr_att[:, cols(h)]
            kk = lk[:, cols(h)]
            dlq[:, cols(h)] = (nn(gweights[h], kk) + lead_s[h] * nt(da, car[0, h])).astype(BF16)
            dlk[:, cols(h)] = (
                tn(gweights[h], lq[:, cols(h)]) + tail_s[h] * nt(lv[:, cols(h)], car[1, h])
            ).astype(BF16)
            dlv[:, cols(h)] = (tn(weights[h], da) + tail_s[h] * nn(kk, car[1, h])).astype(BF16)

    def fwd_tile(h, keys, values_t, key_start):
        s = nn(keys, q_t[h])
        if key_start is not None:
            key_at = key_start + lax.broadcasted_iota(jnp.int32, s.shape, 0)
            query_at = y * TOK + lax.broadcasted_iota(jnp.int32, s.shape, 1)
            s = jnp.where(key_at <= query_at, s, NEG)
        old = peak[h]
        new = jnp.maximum(old, jnp.max(s, axis=0, keepdims=True))
        shrink = jnp.exp2((old - new) * EXP_SCALE)
        p = jnp.exp2((s - new) * EXP_SCALE)
        peak[h] = new
        total[h] = total[h] * shrink + jnp.sum(p, axis=0, keepdims=True)
        out_t[h] = out_t[h] * shrink + nn(values_t, p.astype(BF16))

    def fwd_row(d):
        rows = row_at(z - d)
        v_t[...] = vall[rows, :].T

        def head(h, c):
            fwd_tile(h, kall[rows, :], v_t[...], None)
            return c

        lax.fori_loop(0, HEADS, head, 0)

    def fwd_diagonal():
        for h in range(HEADS):
            peak[h] = jnp.full((1, TOK), NEG, F32)
            total[h] = jnp.zeros((1, TOK), F32)
            out_t[h] = jnp.zeros((DH, TOK), F32)

        def one(i, c):
            yy = y - i
            rows = block_at(z, yy)
            v_t[:, :TOK] = vall[rows, :].T

            def head(h, c):
                fwd_tile(h, kall[rows, :], v_t[:, :TOK], yy * TOK)
                return c

            return lax.fori_loop(0, HEADS, head, c)

        lax.fori_loop(0, y + 1, one, 0)

    def finish_forward():
        for h in range(HEADS):
            o = (out_t[h] / total[h]).astype(BF16)
            sout[:, cols(h)] = o.T
            delta_s[h] = jnp.sum(g_t[h].astype(F32) * o.astype(F32), axis=0, keepdims=True)
            log_s[h] = peak[h] * EXP_SCALE + jnp.log(total[h]) * LOG2E
            dq_t[h] = jnp.zeros((DH, TOK), F32)

    def bwd_tile(h, keys, values, keys_t, key_start):
        s = nn(keys, q_t[h])
        p = jnp.exp2(s * EXP_SCALE - log_s[h])
        if key_start is not None:
            key_at = key_start + lax.broadcasted_iota(jnp.int32, s.shape, 0)
            query_at = y * TOK + lax.broadcasted_iota(jnp.int32, s.shape, 1)
            p = jnp.where(key_at <= query_at, p, 0.0)
        dp = nn(values, g_t[h])
        ds = (p * (dp - delta_s[h])).astype(BF16)
        dq_t[h] = dq_t[h] + nn(keys_t, ds)
        at = pl.ds(pl.multiple_of(h * DH, DH), DH)
        return nn(ds, sq[:, at]), nn(p.astype(BF16), so[:, at])

    def bwd_row(d):
        rows = row_at(z - d)
        k_t[...] = kall[rows, :].T
        dk_acc[...] = jnp.zeros((ROW, DH), F32)
        dv_acc[...] = jnp.zeros((ROW, DH), F32)

        def head(h, c):
            dk, dv = bwd_tile(h, kall[rows, :], vall[rows, :], k_t[...], None)
            dk_acc[...] = dk_acc[...] + dk
            dv_acc[...] = dv_acc[...] + dv
            return c

        lax.fori_loop(0, HEADS, head, 0)

    def local_block(yy):
        return pl.ds(pl.multiple_of(yy * TOK, TOK), TOK)

    def bwd_diagonal():
        dk_acc[...] = jnp.zeros((ROW, DH), F32)
        dv_acc[...] = jnp.zeros((ROW, DH), F32)

        def one(yy, c):
            rows = block_at(z, yy)
            own = local_block(yy)
            k_t[:, :TOK] = kall[rows, :].T

            def head(h, c):
                dk, dv = bwd_tile(h, kall[rows, :], vall[rows, :], k_t[:, :TOK], yy * TOK)
                dk_acc[own, :] = dk_acc[own, :] + dk
                dv_acc[own, :] = dv_acc[own, :] + dv
                return c

            return lax.fori_loop(0, HEADS, head, c)

        lax.fori_loop(0, y + 1, one, 0)

    def target(d):
        near = d <= 4
        to_z = jnp.where(near, z - 1, jnp.where(up, z + 1, z - d))
        slot = jnp.where(near, d - 1, jnp.where(up, d + 1, 4))
        return to_z, slot

    def has_incoming(d):
        return ((d <= 3) & up) | (d >= 6)

    def dk_copy(d):
        to_z, slot = target(d)
        return copy(dks.at[d], dkr.at[slot], dk_s.at[d], dk_r.at[slot], at_ctx(to_z, y))

    def dv_copy(d):
        to_z, slot = target(d)
        return copy(dvz.at[d], dvr.at[slot], dv_s.at[d], dv_r.at[slot], at_ctx(to_z, y))

    def dv_to_peer(d, j):
        at = d * 3 + j - 1
        src = dvs.at[d, local_block(y_peer(j))]
        return copy(src, dvy.at[d, j], dvy_s.at[at], dvy_r.at[at], at_ctx(z, y_peer(j)))

    def dk_to_peer(j):
        src = dks.at[0, local_block(y_peer(j))]
        return copy(src, dky.at[j], dky_s.at[j - 1], dky_r.at[j - 1], at_ctx(z, y_peer(j)))

    def spread_dv(d):
        dvs[d] = dv_acc[...].astype(BF16)
        dv_own[d] = dv_acc[local_block(y), :]
        for j in range(1, NY):
            dv_to_peer(d, j).start()

    def own_dv(d):
        acc = dv_own[d]
        for j in range(1, NY):
            at = d * 3 + j - 1
            arrived(dvy.at[d, j], dvy_r.at[at], dvy_s.at[at])
            acc = acc + dvy[d, j].astype(F32)
        return acc

    def add_incoming(acc, slots, sems, others, slot):
        arrived(slots.at[slot], sems.at[slot], others.at[slot])
        acc[...] = acc[...] + slots[slot].astype(F32)

    def pass_dk(d):
        @pl.when(has_incoming(d))
        def _():
            add_incoming(dk_acc, dkr, dk_r, dk_s, d)

        dks[d] = dk_acc[...].astype(BF16)
        dk_copy(d).start()

    part = dv_acc.at[pl.ds(0, TOK)]

    def pass_dv(d):
        @pl.when(z >= d)
        def _():
            part[...] = own_dv(d)

            @pl.when(has_incoming(d))
            def _():
                add_incoming(part, dvr, dv_r, dv_s, d)

            dvz[d] = part[...].astype(BF16)
            dv_copy(d).start()

    def fwd_order(t):
        return jnp.where(lax.rem(t, 2) == 1, lax.div(t + 1, 2), NZ - lax.div(t, 2))

    def bwd_order(t):
        return jnp.where(lax.rem(t, 2) == 0, 4 - lax.div(t, 2), 5 + lax.div(t - 1, 2))

    fetch(1)
    peer_values(0)
    fwd_diagonal()

    events = (
        lambda: join_row(0),
        lambda: join_all(0),
        attend,
        norm_and_grad,
        lambda: join_row(1),
        lambda: join_all(1),
        lin_grads,
    )

    def fwd_step(t, c):
        d = fwd_order(t)

        @pl.when(t < NZ - 1)
        def _():
            fetch(fwd_order(t + 1))

        @pl.when(z >= d)
        def _():
            peer_values(d)
            fwd_row(d)

        for i, event in enumerate(events):
            pl.when(t == i + 1)(event)
        return c

    lax.fori_loop(1, NZ, fwd_step, 0)
    finish_forward()

    def bwd_step(t, c):
        d = bwd_order(t)

        @pl.when(z >= d)
        def _():
            bwd_row(d)
            spread_dv(d)
            pass_dk(d)

        @pl.when(t > 0)
        def _():
            pass_dv(bwd_order(t - 1))

        return c

    lax.fori_loop(0, NZ - 1, bwd_step, 0)
    bwd_diagonal()
    spread_dv(0)

    @pl.when(up)
    def _():
        add_incoming(dk_acc, dkr, dk_r, dk_s, 0)

    @pl.when(low)
    def _():
        add_incoming(dk_acc, dkr, dk_r, dk_s, 4)

    dks[0] = dk_acc[...].astype(BF16)
    for j in range(1, NY):
        dk_to_peer(j).start()
    pass_dv(1)
    for h in range(HEADS):
        dsq[:, cols(h)] = (dq_t[h] * SCALE).T.astype(BF16)
    part[...] = own_dv(0)

    @pl.when(up)
    def _():
        add_incoming(part, dvr, dv_r, dv_s, 0)

    @pl.when(low)
    def _():
        add_incoming(part, dvr, dv_r, dv_s, 4)

    dsv[...] = part[...].astype(BF16)
    acc = dk_acc[local_block(y), :]
    for j in range(1, NY):
        arrived(dky.at[j], dky_r.at[j - 1], dky_s.at[j - 1])
        acc = acc + dky[j].astype(F32)
    dsk[...] = (acc * SCALE).astype(BF16)

    for j in range(1, NY):
        key_to_peer(j).wait_send()
        dk_to_peer(j).wait_send()
        for k in range(2):
            state_to_peer(k, j).wait_send()
            carried_to_peer(k, j).wait_send()
    for j in range(1, NT):
        sums_to(j).wait_send()
    for k in range(2):

        def gone(zz, c, k=k):
            total_to(k, zz).wait_send()
            return c

        lax.fori_loop(*z_targets(k), gone, 0)

    @pl.when(low)
    def _():
        value_to(0, last, last - z, 4).wait_send()
        row_to(0, last, last - z, 4).wait_send()

    def all_gone(d, c):
        @pl.when(z >= d)
        def _():
            @pl.when((d <= 3) & up)
            def _():
                value_to(d, z + 1, d + 1, d).wait_send()
                row_to(d, z + 1, d + 1, d).wait_send()

            @pl.when(d >= 6)
            def _():
                value_to(d, z - 1, d - 1, d).wait_send()
                row_to(d, z - 1, d - 1, d).wait_send()

            for j in range(1, NY):
                value_to_peer(d, j).wait_send()
                dv_to_peer(d, j).wait_send()

            @pl.when(d >= 1)
            def _():
                dk_copy(d).wait_send()
                dv_copy(d).wait_send()

        return c

    lax.fori_loop(0, NZ, all_gone, 0)


def body(lin_query, lin_key, lin_value, log_decay, norm_gain, lin_gate, lin_grad, soft_query, soft_key, soft_value, soft_grad):
    wide = jax.ShapeDtypeStruct((TOK, HEADS * DH), BF16)
    narrow = jax.ShapeDtypeStruct((TOK, DH), BF16)
    dma = pltpu.SemaphoreType.DMA
    vmem = pltpu.VMEM
    scratch = [
        vmem((NZ * ROW, DH), BF16),
        vmem((NZ * ROW, DH), BF16),
        vmem((HEADS, DH, TOK), BF16),
        vmem((HEADS, DH, TOK), BF16),
        vmem((DH, ROW), BF16),
        vmem((DH, ROW), BF16),
        vmem((HEADS, 1, TOK), F32),
        vmem((HEADS, 1, TOK), F32),
        vmem((HEADS, DH, TOK), F32),
        vmem((HEADS, 1, TOK), F32),
        vmem((HEADS, 1, TOK), F32),
        vmem((HEADS, DH, TOK), F32),
        vmem((ROW, DH), F32),
        vmem((ROW, DH), F32),
        vmem((NZ, ROW, DH), BF16),
        vmem((NZ, ROW, DH), BF16),
        vmem((NZ, ROW, DH), BF16),
        vmem((NZ, NY, TOK, DH), BF16),
        vmem((NZ, TOK, DH), F32),
        vmem((NZ, TOK, DH), BF16),
        vmem((NZ, TOK, DH), BF16),
        vmem((NY, TOK, DH), BF16),
        vmem((HEADS, TOK, TOK), F32),
        vmem((HEADS, TOK, TOK), BF16),
        vmem((HEADS, TOK, TOK), BF16),
        vmem((HEADS, TOK, DH), F32),
        vmem((HEADS, TOK, DH), F32),
        vmem((TOK, HEADS * DH), F32),
        vmem((TOK, HEADS * DH), BF16),
        vmem((2, HEADS, MSG, DH), BF16),
        vmem((2, NY, MSG, DH), BF16),
        vmem((NY, DH, DH), F32),
        vmem((NY, 1, DH), F32),
        vmem((2, MSG, DH), BF16),
        vmem((2, NZ, MSG, DH), BF16),
        vmem((2, NY, DH, DH), BF16),
        vmem((2, HEADS, DH, DH), BF16),
        vmem((16, TOK), F32),
        vmem((NT, 16, TOK), F32),
        dma((3,)), dma((3,)),
        dma((NZ,)), dma((NZ,)),
        dma((NZ,)), dma((NZ,)),
        dma((3 * NZ,)), dma((3 * NZ,)),
        dma((6,)), dma((6,)),
        dma((2 * NZ,)), dma((2 * NZ,)),
        dma((6,)), dma((6,)),
        dma((NT - 1,)), dma((NT - 1,)),
        dma((NZ,)), dma((NZ,)),
        dma((NZ,)), dma((NZ,)),
        dma((3 * NZ,)), dma((3 * NZ,)),
        dma((3,)), dma((3,)),
    ]
    return pl.pallas_call(
        kernel,
        out_shape=[wide] * 7 + [narrow] * 2,
        in_specs=[pl.BlockSpec(memory_space=pltpu.VMEM)] * 11,
        out_specs=[pl.BlockSpec(memory_space=pltpu.VMEM)] * 9,
        scratch_shapes=scratch,
        compiler_params=pltpu.CompilerParams(
            collective_id=0, has_side_effects=True, vmem_limit_bytes=56 * 2**20
        ),
    )(
        lin_query, lin_key, lin_value, log_decay, norm_gain.reshape(1, -1), lin_gate, lin_grad,
        soft_query, soft_key, soft_value, soft_grad,
    )


def solution(mesh):
    shared = P("ctx", "tp")
    return jax.shard_map(
        lambda *args: tuple(body(*args)),
        mesh=mesh,
        in_specs=(shared, shared, shared, P("tp", "ctx"), P("tp"), shared, shared, shared, shared, shared, shared),
        out_specs=(shared,) * 9,
        check_vma=False,
    )
```

```python
import math

import jax
import jax.numpy as jnp
from jax import lax
from jax.experimental import pallas as pl
from jax.experimental.pallas import tpu as pltpu
from jax.sharding import PartitionSpec as P

DH = 128
HEADS = 4
TOK = 256
NY = 4
NZ = 8
NT = 8
ROW = NY * TOK
WIDTH = 4096
MSG = DH + 16
F32 = jnp.float32
BF16 = jnp.bfloat16
MESH = pl.DeviceIdType.MESH
SCALE = DH ** (-0.5)
LOG2E = math.log2(math.e)
EXP_SCALE = SCALE * LOG2E
NEG = -1e30
EXACT = lax.Precision.HIGHEST


def nn(a, b, precision=None):
    return lax.dot_general(a, b, (((1,), (0,)), ((), ())), precision=precision, preferred_element_type=F32)


def nt(a, b, precision=None):
    return lax.dot_general(a, b, (((1,), (1,)), ((), ())), precision=precision, preferred_element_type=F32)


def tn(a, b, precision=None):
    return lax.dot_general(a, b, (((0,), (0,)), ((), ())), precision=precision, preferred_element_type=F32)


def cols(h):
    return slice(h * DH, (h + 1) * DH)


def kernel(
    lq, lk, lv, ld, gain, gate, lgrad, sq, sk, sv, so,
    lin_out, dlq, dlk, dlv, dgate, sout, dsq, dsk, dsv,
    kall, vall, q_t, g_t, v_t, k_t, peak, total, out_t, log_s, delta_s, dq_t, dk_acc, dv_acc,
    dks, dkr, dvs, dvy, dv_own, dvz, dvr, dky,
    decay, weights, gweights, tail_s, lead_s, att, gr_att, msg, st, pre, lead_tot, rmsg, rst, cmsg, car, tps, tpr,
    ky_s, ky_r, ks_s, kr_r, vs_s, vr_r, vy_s, vy_r, p1_s, p1_r, p2_s, p2_r, p3_s, p3_r, tp_s, tp_r,
    dk_s, dk_r, dv_s, dv_r, dvy_s, dvy_r, dky_s, dky_r,
):
    ctx = lax.axis_index("ctx")
    tp = lax.axis_index("tp")
    z = lax.div(ctx, NY)
    y = lax.rem(ctx, NY)

    def at_ctx(zz, yy):
        return {"ctx": zz * NY + yy}

    def y_peer(j):
        return lax.rem(y + j, NY)

    def y_from(j):
        return lax.rem(y + NY - j, NY)

    def copy(src, dst, s, r, device):
        return pltpu.make_async_remote_copy(
            src_ref=src, dst_ref=dst, send_sem=s, recv_sem=r, device_id=device, device_id_type=MESH
        )

    neighbour = at_ctx(z, y_peer(1))

    def arrived(dst, r, s):
        copy(dst, dst, s, r, neighbour).wait_recv()

    def sent(src, s, r):
        copy(src, src, s, r, neighbour).wait_send()

    barrier = pltpu.get_barrier_semaphore()
    for j in range(1, NY):
        pl.semaphore_signal(barrier, inc=1, device_id=at_ctx(z, y_peer(j)), device_id_type=MESH)
    for j in range(1, NZ):
        pl.semaphore_signal(barrier, inc=1, device_id=at_ctx(lax.rem(z + j, NZ), y), device_id_type=MESH)
    for j in range(1, NT):
        pl.semaphore_signal(barrier, inc=1, device_id={"tp": lax.rem(tp + j, NT)}, device_id_type=MESH)
    pl.semaphore_wait(barrier, NY + NZ + NT - 3)

    def block_at(zz, yy):
        return pl.ds(pl.multiple_of((zz * NY + yy) * TOK, TOK), TOK)

    def row_at(zz):
        return pl.ds(pl.multiple_of(zz * ROW, ROW), ROW)

    def key_to_peer(j):
        return copy(sk, kall.at[block_at(z, y)], ky_s.at[j - 1], ky_r.at[j - 1], at_ctx(z, y_peer(j)))

    def value_to_peer(d, j):
        ref = vall.at[block_at(z - d, y)]
        at = d * 3 + j - 1
        return copy(ref, ref, vy_s.at[at], vy_r.at[at], at_ctx(z, y_peer(j)))

    up = z < NZ - 1
    low = z <= 2

    def rem_z(zz):
        return lax.rem(zz + NZ, NZ)

    def half_of(zz, half):
        return pl.ds(pl.multiple_of(zz * ROW + half * (ROW // 2), ROW // 2), ROW // 2)

    def row_to(zz, to_z, step, half):
        ref = kall.at[half_of(zz, half)]
        at = step * 2 + half
        return copy(ref, ref, ks_s.at[at], kr_r.at[at], at_ctx(to_z, y))

    def value_to(zz, to_z, step):
        ref = vall.at[block_at(zz, y)]
        return copy(ref, ref, vs_s.at[step], vr_r.at[step], at_ctx(to_z, y))

    def upward(s, act, more):
        pl.when(up & more)(lambda: act(z - s, z + 1, s + 1))

    def downward(s, act, more):
        pl.when(more)(lambda: act(rem_z(z + s), rem_z(z - 1), s + 5))

    def fetch_values(s):
        @pl.when(z >= s)
        def _():
            arrived(vall.at[block_at(z - s, y)], vr_r.at[s], vs_s.at[s])
            upward(s, lambda *a: value_to(*a).start(), s < 4)
            for j in range(1, NY):
                value_to_peer(s, j).start()

        @pl.when((s <= 3) & (rem_z(z + s) <= 2))
        def _():
            arrived(vall.at[block_at(rem_z(z + s), y)], vr_r.at[s + 4], vs_s.at[s + 4])
            downward(s, lambda *a: value_to(*a).start(), s < 3)

            @pl.when(z + s >= NZ)
            def _():
                for j in range(1, NY):
                    value_to_peer(NZ - s, j).start()

    def fetch_keys(s, half):
        @pl.when(z >= s)
        def _():
            at = s * 2 + half
            arrived(kall.at[half_of(z - s, half)], kr_r.at[at], ks_s.at[at])
            upward(s, lambda *a: row_to(*a, half).start(), s < 4)

        @pl.when((s <= 3) & (rem_z(z + s) <= 2))
        def _():
            at = (s + 4) * 2 + half
            arrived(kall.at[half_of(rem_z(z + s), half)], kr_r.at[at], ks_s.at[at])
            downward(s, lambda *a: row_to(*a, half).start(), s < 3)

    def peer_values(d):
        for j in range(1, NY):
            at = d * 3 + j - 1
            arrived(vall.at[block_at(z - d, y_from(j))], vy_r.at[at], vy_s.at[at])

    kall[block_at(z, y), :] = sk[...]
    vall[block_at(z, y), :] = sv[...]
    for j in range(1, NY):
        key_to_peer(j).start()

    upward(0, lambda *a: value_to(*a).start(), True)
    downward(0, lambda *a: value_to(*a).start(), low)
    for j in range(1, NY):
        value_to_peer(0, j).start()

    for h in range(HEADS):
        q_t[h] = sq[:, cols(h)].T
        g_t[h] = so[:, cols(h)].T

    for j in range(1, NY):
        arrived(kall.at[block_at(z, y_from(j))], ky_r.at[j - 1], ky_s.at[j - 1])

    for half in range(2):
        upward(0, lambda *a: row_to(*a, half).start(), True)
        downward(0, lambda *a: row_to(*a, half).start(), low)

    def coded(tot):
        first = tot.astype(BF16).astype(F32)
        second = (tot - first).astype(BF16).astype(F32)
        third = (tot - first - second).astype(BF16).astype(F32)
        r = lax.broadcasted_iota(jnp.int32, (16, DH), 0)
        rows = jnp.where(r == 0, first, jnp.where(r == 1, second, jnp.where(r == 2, third, 0.0)))
        return rows.astype(BF16)

    def decoded(rows):
        return jnp.sum(rows.astype(F32), axis=0, keepdims=True)

    def state_to_peer(k, j):
        at = k * 3 + j - 1
        return copy(msg.at[k, y_peer(j)], st.at[k, y], p1_s.at[at], p1_r.at[at], at_ctx(z, y_peer(j)))

    def total_to(k, zz):
        return copy(rmsg.at[k], rst.at[k, z], p2_s.at[k * NZ + zz], p2_r.at[k * NZ + z], at_ctx(zz, y))

    def carried_to_peer(k, j):
        at = k * 3 + j - 1
        return copy(cmsg.at[k, y_peer(j)], car.at[k, y], p3_s.at[at], p3_r.at[at], at_ctx(z, y_peer(j)))

    def send_states(k):
        st[k, y] = msg[k, y]
        for j in range(1, NY):
            state_to_peer(k, j).start()

    def z_targets(k):
        return (z + 1, NZ) if k == 0 else (0, z)

    def join_row(k):
        for j in range(1, NY):
            at = k * 3 + j - 1
            arrived(st.at[k, y_from(j)], p1_r.at[at], p1_s.at[at])
        order = range(NY) if k == 0 else range(NY - 1, -1, -1)
        state = jnp.zeros((DH, DH), F32)
        so_far = jnp.zeros((1, DH), F32)
        for i in order:
            pre[i] = state
            lead_tot[i] = so_far
            tot = decoded(st[k, i, DH:, :])
            state = jnp.exp(tot) * state + st[k, i, :DH, :].astype(F32)
            so_far = so_far + tot
        rmsg[k, :DH, :] = state.astype(BF16)
        rmsg[k, DH:, :] = coded(so_far)

        def one(zz, c):
            total_to(k, zz).start()
            return c

        lax.fori_loop(*z_targets(k), one, 0)

    def join_all(k):
        def one(i, state):
            zz = i if k == 0 else NZ - 1 - i
            at = k * NZ + zz
            arrived(rst.at[k, zz], p2_r.at[at], p2_s.at[at])
            return jnp.exp(decoded(rst[k, zz, DH:, :])) * state + rst[k, zz, :DH, :].astype(F32)

        state = lax.fori_loop(0, z if k == 0 else NZ - 1 - z, one, jnp.zeros((DH, DH), F32))
        for i in range(NY):
            cmsg[k, i] = (pre[i] + jnp.exp(lead_tot[i]) * state).astype(BF16)
        car[k, y] = cmsg[k, y]
        for j in range(1, NY):
            carried_to_peer(k, j).start()

    def take_carried(k):
        for j in range(1, NY):
            at = k * 3 + j - 1
            arrived(car.at[k, y_from(j)], p3_r.at[at], p3_s.at[at])

    logs = jnp.concatenate([ld[...], jnp.zeros((8 - HEADS, TOK), F32)], axis=0)
    earlier = lax.broadcasted_iota(jnp.int32, (TOK, TOK), 0)
    later = lax.broadcasted_iota(jnp.int32, (TOK, TOK), 1)
    log_rows = nn(logs, (earlier <= later).astype(F32), EXACT)
    log_cols = nt((later <= earlier).astype(F32), logs, EXACT)
    causal = earlier >= later
    for h in range(HEADS):
        col = log_cols[:, h : h + 1]
        row = log_rows[h : h + 1, :]
        tot = log_rows[h : h + 1, TOK - 1 :]
        dec = jnp.exp(jnp.where(causal, col - row, NEG))
        decay[h] = dec
        tail = jnp.broadcast_to(jnp.exp(tot - col), (TOK, DH))
        tail_s[h] = tail
        lead_s[h] = jnp.broadcast_to(jnp.exp(col), (TOK, DH))
        kk = lk[:, cols(h)]
        weights[h] = (nt(lq[:, cols(h)], kk) * dec).astype(BF16)
        msg[0, h, :DH, :] = tn((kk.astype(F32) * tail).astype(BF16), lv[:, cols(h)]).astype(BF16)
        code = coded(jnp.broadcast_to(tot, (1, DH)))
        msg[0, h, DH:, :] = code
        msg[1, h, DH:, :] = code
    send_states(0)

    def gated(h):
        sig = jax.nn.sigmoid(gate[:, cols(h)].astype(F32))
        return sig, gain[:, cols(h)], lgrad[:, cols(h)].astype(F32)

    def sums_to(j):
        return copy(tps, tpr.at[j], tp_s.at[j - 1], tp_r.at[j - 1], {"tp": lax.rem(tp + j, NT)})

    def attend():
        take_carried(0)
        squares = jnp.zeros((TOK, DH), F32)
        cross = jnp.zeros((TOK, DH), F32)
        for h in range(HEADS):
            a = nn(weights[h], lv[:, cols(h)]) + lead_s[h] * nn(lq[:, cols(h)], car[0, h])
            att[:, cols(h)] = a
            sig, gn, gr = gated(h)
            squares = squares + a * a
            cross = cross + gr * gn * sig * a
        ones = jnp.ones((8, DH), F32)
        tps[0:8, :] = nt(ones, squares, EXACT)
        tps[8:16, :] = nt(ones, cross, EXACT)
        for j in range(1, NT):
            sums_to(j).start()

    def norm_and_grad():
        tot = tps[...]
        for j in range(1, NT):
            arrived(tpr.at[j], tp_r.at[j - 1], tp_s.at[j - 1])
            tot = tot + tpr[j]
        rms_row = lax.rsqrt(tot[0:8] / WIDTH + 1e-05)
        mean_row = rms_row * tot[8:16] / WIDTH
        eye = (earlier == later).astype(F32)
        rms = nt(eye, rms_row, EXACT)[:, 0:1]
        mean = nt(eye, mean_row, EXACT)[:, 0:1]
        for h in range(HEADS):
            sig, gn, gr = gated(h)
            normed = att[:, cols(h)] * rms
            by_gain = normed * gn * sig
            lin_out[:, cols(h)] = by_gain.astype(BF16)
            dgate[:, cols(h)] = (gr * by_gain * (1.0 - sig)).astype(BF16)
            da = (rms * (gr * gn * sig - normed * mean)).astype(BF16)
            gr_att[:, cols(h)] = da
            gweights[h] = (nt(da, lv[:, cols(h)]) * decay[h]).astype(BF16)
            msg[1, h, :DH, :] = tn((lq[:, cols(h)].astype(F32) * lead_s[h]).astype(BF16), da).astype(BF16)
        send_states(1)

    def lin_grads():
        take_carried(1)
        for h in range(HEADS):
            da = gr_att[:, cols(h)]
            kk = lk[:, cols(h)]
            dlq[:, cols(h)] = (nn(gweights[h], kk) + lead_s[h] * nt(da, car[0, h])).astype(BF16)
            dlk[:, cols(h)] = (
                tn(gweights[h], lq[:, cols(h)]) + tail_s[h] * nt(lv[:, cols(h)], car[1, h])
            ).astype(BF16)
            dlv[:, cols(h)] = (tn(weights[h], da) + tail_s[h] * nn(kk, car[1, h])).astype(BF16)

    def fwd_tile(h, keys, values_t, key_start):
        s = nn(keys, q_t[h])
        if key_start is not None:
            key_at = key_start + lax.broadcasted_iota(jnp.int32, s.shape, 0)
            query_at = y * TOK + lax.broadcasted_iota(jnp.int32, s.shape, 1)
            s = jnp.where(key_at <= query_at, s, NEG)
        old = peak[h]
        new = jnp.maximum(old, jnp.max(s, axis=0, keepdims=True))
        shrink = jnp.exp2((old - new) * EXP_SCALE)
        p = jnp.exp2((s - new) * EXP_SCALE)
        peak[h] = new
        total[h] = total[h] * shrink + jnp.sum(p, axis=0, keepdims=True)
        out_t[h] = out_t[h] * shrink + nn(values_t, p.astype(BF16))

    def fwd_row(d):
        rows = row_at(z - d)
        v_t[...] = vall[rows, :].T

        for h in range(HEADS):
            fwd_tile(h, kall[rows, :], v_t[...], None)

    def fwd_diagonal():
        for h in range(HEADS):
            peak[h] = jnp.full((1, TOK), NEG, F32)
            total[h] = jnp.zeros((1, TOK), F32)
            out_t[h] = jnp.zeros((DH, TOK), F32)

        rows = row_at(z)
        v_t[...] = vall[rows, :].T
        for h in range(HEADS):
            fwd_tile(h, kall[rows, :], v_t[...], 0)

    def finish_forward():
        for h in range(HEADS):
            o = (out_t[h] / total[h]).astype(BF16)
            sout[:, cols(h)] = o.T
            delta_s[h] = jnp.sum(g_t[h].astype(F32) * o.astype(F32), axis=0, keepdims=True)
            log_s[h] = peak[h] * EXP_SCALE + jnp.log(total[h]) * LOG2E
            dq_t[h] = jnp.zeros((DH, TOK), F32)

    def bwd_tile(h, keys, values, keys_t, key_start):
        s = nn(keys, q_t[h])
        p = jnp.exp2(s * EXP_SCALE - log_s[h])
        if key_start is not None:
            key_at = key_start + lax.broadcasted_iota(jnp.int32, s.shape, 0)
            query_at = y * TOK + lax.broadcasted_iota(jnp.int32, s.shape, 1)
            p = jnp.where(key_at <= query_at, p, 0.0)
        dp = nn(values, g_t[h])
        ds = (p * (dp - delta_s[h])).astype(BF16)
        dq_t[h] = dq_t[h] + nn(keys_t, ds)
        return nn(ds, sq[:, cols(h)]), nn(p.astype(BF16), so[:, cols(h)])

    def bwd_row(d, start=None):
        rows = row_at(z - d)
        k_t[...] = kall[rows, :].T

        for h in range(HEADS):
            dk, dv = bwd_tile(h, kall[rows, :], vall[rows, :], k_t[...], start)
            dk_acc[...] = dk if h == 0 else dk_acc[...] + dk
            dv_acc[...] = dv if h == 0 else dv_acc[...] + dv

    def local_block(yy):
        return pl.ds(pl.multiple_of(yy * TOK, TOK), TOK)

    def target(d):
        near = d <= 4
        to_z = jnp.where(near, z - 1, jnp.where(up, z + 1, z - d))
        slot = jnp.where(near, d - 1, jnp.where(up, d + 1, 4))
        return to_z, slot

    def has_incoming(d):
        return ((d <= 3) & up) | (d >= 6)

    def dk_copy(d):
        to_z, slot = target(d)
        return copy(dks.at[d], dkr.at[slot], dk_s.at[d], dk_r.at[slot], at_ctx(to_z, y))

    def dv_copy(d):
        to_z, slot = target(d)
        return copy(dvz.at[d], dvr.at[slot], dv_s.at[d], dv_r.at[slot], at_ctx(to_z, y))

    def dv_to_peer(d, j):
        at = d * 3 + j - 1
        src = dvs.at[d, local_block(y_peer(j))]
        return copy(src, dvy.at[d, j], dvy_s.at[at], dvy_r.at[at], at_ctx(z, y_peer(j)))

    def dk_to_peer(j):
        src = dks.at[0, local_block(y_peer(j))]
        return copy(src, dky.at[j], dky_s.at[j - 1], dky_r.at[j - 1], at_ctx(z, y_peer(j)))

    def spread_dv(d):
        dvs[d] = dv_acc[...].astype(BF16)
        dv_own[d] = dv_acc[local_block(y), :]
        for j in range(1, NY):
            dv_to_peer(d, j).start()

    def own_dv(d):
        acc = dv_own[d]
        for j in range(1, NY):
            at = d * 3 + j - 1
            arrived(dvy.at[d, j], dvy_r.at[at], dvy_s.at[at])
            acc = acc + dvy[d, j].astype(F32)
        return acc

    def add_incoming(acc, slots, sems, others, slot):
        arrived(slots.at[slot], sems.at[slot], others.at[slot])
        acc[...] = acc[...] + slots[slot].astype(F32)

    def pass_dk(d):
        @pl.when(has_incoming(d))
        def _():
            add_incoming(dk_acc, dkr, dk_r, dk_s, d)

        dks[d] = dk_acc[...].astype(BF16)
        dk_copy(d).start()

    part = dv_acc.at[pl.ds(0, TOK)]

    def pass_dv(d):
        @pl.when(z >= d)
        def _():
            part[...] = own_dv(d)

            @pl.when(has_incoming(d))
            def _():
                add_incoming(part, dvr, dv_r, dv_s, d)

            dvz[d] = part[...].astype(BF16)
            dv_copy(d).start()

    def bwd_order(t):
        return jnp.where(lax.rem(t, 2) == 0, 4 - lax.div(t, 2), 5 + lax.div(t - 1, 2))

    fetch_values(1)
    fetch_keys(1, 0)
    peer_values(0)
    fwd_diagonal()
    fetch_keys(1, 1)

    def at_steps(now, events):
        for at, event in events:
            pl.when(now == at)(event)

    def fwd_step(s, c):
        @pl.when(s < 4)
        def _():
            fetch_values(s + 1)
            fetch_keys(s + 1, 0)

        @pl.when(z >= s)
        def _():
            peer_values(s)
            fwd_row(s)

        at_steps(s, [(1, lambda: join_row(0)), (3, attend)])

        @pl.when(s < 4)
        def _():
            fetch_keys(s + 1, 1)

            @pl.when(z + s >= NZ)
            def _():
                peer_values(NZ - s)
                fwd_row(NZ - s)

        at_steps(s, [(2, lambda: join_all(0)), (4, norm_and_grad)])
        return c

    lax.fori_loop(1, 5, fwd_step, 0)
    finish_forward()

    def bwd_step(t, c):
        d = bwd_order(t)

        @pl.when(z >= d)
        def _():
            bwd_row(d)
            spread_dv(d)
            pass_dk(d)

        @pl.when(t > 0)
        def _():
            pass_dv(bwd_order(t - 1))

        at_steps(t, [(1, lambda: join_row(1)), (3, lambda: join_all(1)), (5, lin_grads)])
        return c

    lax.fori_loop(0, NZ - 1, bwd_step, 0)
    bwd_row(0, 0)
    spread_dv(0)

    @pl.when(up)
    def _():
        add_incoming(dk_acc, dkr, dk_r, dk_s, 0)

    @pl.when(low)
    def _():
        add_incoming(dk_acc, dkr, dk_r, dk_s, 4)

    dks[0] = dk_acc[...].astype(BF16)
    for j in range(1, NY):
        dk_to_peer(j).start()
    pass_dv(1)
    for h in range(HEADS):
        dsq[:, cols(h)] = (dq_t[h] * SCALE).T.astype(BF16)
    part[...] = own_dv(0)

    @pl.when(up)
    def _():
        add_incoming(part, dvr, dv_r, dv_s, 0)

    @pl.when(low)
    def _():
        add_incoming(part, dvr, dv_r, dv_s, 4)

    dsv[...] = part[...].astype(BF16)
    acc = dk_acc[local_block(y), :]
    for j in range(1, NY):
        arrived(dky.at[j], dky_r.at[j - 1], dky_s.at[j - 1])
        acc = acc + dky[j].astype(F32)
    dsk[...] = (acc * SCALE).astype(BF16)

    for j in range(1, NY):
        key_to_peer(j).wait_send()
        dk_to_peer(j).wait_send()
        for k in range(2):
            state_to_peer(k, j).wait_send()
            carried_to_peer(k, j).wait_send()
    for j in range(1, NT):
        sums_to(j).wait_send()
    for k in range(2):

        def gone(zz, c, k=k):
            total_to(k, zz).wait_send()
            return c

        lax.fori_loop(*z_targets(k), gone, 0)

    def passed_on(s, c):
        def up_gone(*a):
            value_to(*a).wait_send()
            row_to(*a, 0).wait_send()
            row_to(*a, 1).wait_send()

        pl.when(z >= s)(lambda: upward(s, up_gone, True))
        pl.when((s < 3) & (rem_z(z + s) <= 2))(lambda: downward(s, up_gone, True))
        return c

    lax.fori_loop(0, 4, passed_on, 0)

    def all_gone(d, c):
        @pl.when(z >= d)
        def _():
            for j in range(1, NY):
                value_to_peer(d, j).wait_send()
                dv_to_peer(d, j).wait_send()

            @pl.when(d >= 1)
            def _():
                dk_copy(d).wait_send()
                dv_copy(d).wait_send()

        return c

    lax.fori_loop(0, NZ, all_gone, 0)


def hand_over(*refs):
    for given, made in zip(refs[:9], refs[9:]):
        made[...] = given[...]


def body(lin_query, lin_key, lin_value, log_decay, norm_gain, lin_gate, lin_grad, soft_query, soft_key, soft_value, soft_grad):
    wide = jax.ShapeDtypeStruct((TOK, HEADS * DH), BF16)
    narrow = jax.ShapeDtypeStruct((TOK, DH), BF16)
    dma = pltpu.SemaphoreType.DMA
    vmem = pltpu.VMEM
    scratch = [
        vmem((NZ * ROW, DH), BF16),
        vmem((NZ * ROW, DH), BF16),
        vmem((HEADS, DH, TOK), BF16),
        vmem((HEADS, DH, TOK), BF16),
        vmem((DH, ROW), BF16),
        vmem((DH, ROW), BF16),
        vmem((HEADS, 1, TOK), F32),
        vmem((HEADS, 1, TOK), F32),
        vmem((HEADS, DH, TOK), F32),
        vmem((HEADS, 1, TOK), F32),
        vmem((HEADS, 1, TOK), F32),
        vmem((HEADS, DH, TOK), F32),
        vmem((ROW, DH), F32),
        vmem((ROW, DH), F32),
        vmem((NZ, ROW, DH), BF16),
        vmem((NZ, ROW, DH), BF16),
        vmem((NZ, ROW, DH), BF16),
        vmem((NZ, NY, TOK, DH), BF16),
        vmem((NZ, TOK, DH), F32),
        vmem((NZ, TOK, DH), BF16),
        vmem((NZ, TOK, DH), BF16),
        vmem((NY, TOK, DH), BF16),
        vmem((HEADS, TOK, TOK), F32),
        vmem((HEADS, TOK, TOK), BF16),
        vmem((HEADS, TOK, TOK), BF16),
        vmem((HEADS, TOK, DH), F32),
        vmem((HEADS, TOK, DH), F32),
        vmem((TOK, HEADS * DH), F32),
        vmem((TOK, HEADS * DH), BF16),
        vmem((2, HEADS, MSG, DH), BF16),
        vmem((2, NY, MSG, DH), BF16),
        vmem((NY, DH, DH), F32),
        vmem((NY, 1, DH), F32),
        vmem((2, MSG, DH), BF16),
        vmem((2, NZ, MSG, DH), BF16),
        vmem((2, NY, DH, DH), BF16),
        vmem((2, HEADS, DH, DH), BF16),
        vmem((16, TOK), F32),
        vmem((NT, 16, TOK), F32),
        dma((3,)), dma((3,)),
        dma((2 * NZ,)), dma((2 * NZ,)),
        dma((NZ,)), dma((NZ,)),
        dma((3 * NZ,)), dma((3 * NZ,)),
        dma((6,)), dma((6,)),
        dma((2 * NZ,)), dma((2 * NZ,)),
        dma((6,)), dma((6,)),
        dma((NT - 1,)), dma((NT - 1,)),
        dma((NZ,)), dma((NZ,)),
        dma((NZ,)), dma((NZ,)),
        dma((3 * NZ,)), dma((3 * NZ,)),
        dma((3,)), dma((3,)),
    ]
    shapes = [wide] * 7 + [narrow] * 2
    made = pl.pallas_call(
        kernel,
        out_shape=shapes,
        in_specs=[pl.BlockSpec(memory_space=pltpu.VMEM)] * 11,
        out_specs=[pl.BlockSpec(memory_space=pltpu.VMEM)] * 9,
        scratch_shapes=scratch,
        compiler_params=pltpu.CompilerParams(
            collective_id=0, has_side_effects=True, vmem_limit_bytes=56 * 2**20
        ),
    )(
        lin_query, lin_key, lin_value, log_decay, norm_gain.reshape(1, -1), lin_gate, lin_grad,
        soft_query, soft_key, soft_value, soft_grad,
    )
    whole = pl.BlockSpec(memory_space=pltpu.VMEM)
    return pl.pallas_call(
        hand_over,
        out_shape=shapes,
        in_specs=[whole] * 9,
        out_specs=[whole] * 9,
    )(*made)


def solution(mesh):
    shared = P("ctx", "tp")
    return jax.shard_map(
        lambda *args: tuple(body(*args)),
        mesh=mesh,
        in_specs=(shared, shared, shared, P("tp", "ctx"), P("tp"), shared, shared, shared, shared, shared, shared),
        out_specs=(shared,) * 9,
        check_vma=False,
    )
```

```python
import math

import jax
import jax.numpy as jnp
from jax import lax
from jax.experimental import pallas as pl
from jax.experimental.pallas import tpu as pltpu
from jax.sharding import PartitionSpec as P

DH = 128
HEADS = 4
TOK = 256
NY = 4
NZ = 8
NT = 8
ROW = NY * TOK
WIDTH = 4096
MSG = DH + 16
F32 = jnp.float32
BF16 = jnp.bfloat16
MESH = pl.DeviceIdType.MESH
SCALE = DH ** (-0.5)
LOG2E = math.log2(math.e)
EXP_SCALE = SCALE * LOG2E
NEG = -1e30
EXACT = lax.Precision.HIGHEST


def nn(a, b, precision=None):
    return lax.dot_general(a, b, (((1,), (0,)), ((), ())), precision=precision, preferred_element_type=F32)


def nt(a, b, precision=None):
    return lax.dot_general(a, b, (((1,), (1,)), ((), ())), precision=precision, preferred_element_type=F32)


def tn(a, b, precision=None):
    return lax.dot_general(a, b, (((0,), (0,)), ((), ())), precision=precision, preferred_element_type=F32)


def cols(h):
    return slice(h * DH, (h + 1) * DH)


def kernel(
    lq, lk, lv, ld, gain, gate, lgrad, sq, sk, sv, so,
    lin_out, dlq, dlk, dlv, dgate, sout, dsq, dsk, dsv,
    kall, vall, q_t, g_t, v_t, k_t, peak, total, out_t, log_s, delta_s, dq_t, dk_acc, dv_acc,
    dks, dkr, dvs, dvy, dv_own, dvz, dvr, dky,
    decay, weights, gweights, tail_s, lead_s, att, gr_att, msg, st, pre, lead_tot, row_state, row_tot, before, before_tot, bsum, binc, cmsg, car, tps, tpr,
    ky_s, ky_r, ks_s, kr_r, vs_s, vr_r, vy_s, vy_r, p1_s, p1_r, p2_s, p2_r, p3_s, p3_r, tp_s, tp_r,
    dk_s, dk_r, dv_s, dv_r, dvy_s, dvy_r, dky_s, dky_r,
):
    ctx = lax.axis_index("ctx")
    tp = lax.axis_index("tp")
    z = lax.div(ctx, NY)
    y = lax.rem(ctx, NY)

    def at_ctx(zz, yy):
        return {"ctx": zz * NY + yy}

    def y_peer(j):
        return lax.rem(y + j, NY)

    def y_from(j):
        return lax.rem(y + NY - j, NY)

    def copy(src, dst, s, r, device):
        return pltpu.make_async_remote_copy(
            src_ref=src, dst_ref=dst, send_sem=s, recv_sem=r, device_id=device, device_id_type=MESH
        )

    neighbour = at_ctx(z, y_peer(1))

    def arrived(dst, r, s):
        copy(dst, dst, s, r, neighbour).wait_recv()

    def sent(src, s, r):
        copy(src, src, s, r, neighbour).wait_send()

    barrier = pltpu.get_barrier_semaphore()
    for j in range(1, NY):
        pl.semaphore_signal(barrier, inc=1, device_id=at_ctx(z, y_peer(j)), device_id_type=MESH)
    for j in range(1, NZ):
        pl.semaphore_signal(barrier, inc=1, device_id=at_ctx(lax.rem(z + j, NZ), y), device_id_type=MESH)
    for j in range(1, NT):
        pl.semaphore_signal(barrier, inc=1, device_id={"tp": lax.rem(tp + j, NT)}, device_id_type=MESH)
    pl.semaphore_wait(barrier, NY + NZ + NT - 3)

    def block_at(zz, yy):
        return pl.ds(pl.multiple_of((zz * NY + yy) * TOK, TOK), TOK)

    def row_at(zz):
        return pl.ds(pl.multiple_of(zz * ROW, ROW), ROW)

    def key_to_peer(j):
        return copy(sk, kall.at[block_at(z, y)], ky_s.at[j - 1], ky_r.at[j - 1], at_ctx(z, y_peer(j)))

    def value_to_peer(d, j):
        ref = vall.at[block_at(z - d, y)]
        at = d * 3 + j - 1
        return copy(ref, ref, vy_s.at[at], vy_r.at[at], at_ctx(z, y_peer(j)))

    up = z < NZ - 1
    low = z <= 2

    def rem_z(zz):
        return lax.rem(zz + NZ, NZ)

    def half_of(zz, half):
        return pl.ds(pl.multiple_of(zz * ROW + half * (ROW // 2), ROW // 2), ROW // 2)

    def row_to(zz, to_z, step, half):
        ref = kall.at[half_of(zz, half)]
        at = step * 2 + half
        return copy(ref, ref, ks_s.at[at], kr_r.at[at], at_ctx(to_z, y))

    def value_to(zz, to_z, step):
        ref = vall.at[block_at(zz, y)]
        return copy(ref, ref, vs_s.at[step], vr_r.at[step], at_ctx(to_z, y))

    def upward(s, act, more):
        pl.when(up & more)(lambda: act(z - s, z + 1, s + 1))

    def downward(s, act, more):
        pl.when(more)(lambda: act(rem_z(z + s), rem_z(z - 1), s + 5))

    def fetch_values(s):
        @pl.when(z >= s)
        def _():
            arrived(vall.at[block_at(z - s, y)], vr_r.at[s], vs_s.at[s])
            upward(s, lambda *a: value_to(*a).start(), s < 4)
            for j in range(1, NY):
                value_to_peer(s, j).start()

        @pl.when((s <= 3) & (rem_z(z + s) <= 2))
        def _():
            arrived(vall.at[block_at(rem_z(z + s), y)], vr_r.at[s + 4], vs_s.at[s + 4])
            downward(s, lambda *a: value_to(*a).start(), s < 3)

            @pl.when(z + s >= NZ)
            def _():
                for j in range(1, NY):
                    value_to_peer(NZ - s, j).start()

    def fetch_keys(s, half):
        @pl.when((s <= 4 - half) & (z >= s))
        def _():
            at = s * 2 + half
            arrived(kall.at[half_of(z - s, half)], kr_r.at[at], ks_s.at[at])
            upward(s, lambda *a: row_to(*a, half).start(), s < 4 - half)

        @pl.when((s <= 3 + half) & (rem_z(z + s) <= 2 + half))
        def _():
            at = (s + 4) * 2 + half
            arrived(kall.at[half_of(rem_z(z + s), half)], kr_r.at[at], ks_s.at[at])
            downward(s, lambda *a: row_to(*a, half).start(), s < 3 + half)

    def peer_values(d):
        for j in range(1, NY):
            at = d * 3 + j - 1
            arrived(vall.at[block_at(z - d, y_from(j))], vy_r.at[at], vy_s.at[at])

    kall[block_at(z, y), :] = sk[...]
    vall[block_at(z, y), :] = sv[...]
    for j in range(1, NY):
        key_to_peer(j).start()

    upward(0, lambda *a: value_to(*a).start(), True)
    downward(0, lambda *a: value_to(*a).start(), low)
    for j in range(1, NY):
        value_to_peer(0, j).start()

    for h in range(HEADS):
        q_t[h] = sq[:, cols(h)].T
        g_t[h] = so[:, cols(h)].T

    for j in range(1, NY):
        arrived(kall.at[block_at(z, y_from(j))], ky_r.at[j - 1], ky_s.at[j - 1])

    for half in range(2):
        upward(0, lambda *a: row_to(*a, half).start(), True)
        downward(0, lambda *a: row_to(*a, half).start(), z <= 2 + half)

    def coded(tot):
        first = tot.astype(BF16).astype(F32)
        second = (tot - first).astype(BF16).astype(F32)
        third = (tot - first - second).astype(BF16).astype(F32)
        r = lax.broadcasted_iota(jnp.int32, (16, DH), 0)
        rows = jnp.where(r == 0, first, jnp.where(r == 1, second, jnp.where(r == 2, third, 0.0)))
        return rows.astype(BF16)

    def decoded(rows):
        return jnp.sum(rows.astype(F32), axis=0, keepdims=True)

    def state_to_peer(k, j):
        at = k * 3 + j - 1
        return copy(msg.at[k, y_peer(j)], st.at[k, y], p1_s.at[at], p1_r.at[at], at_ctx(z, y_peer(j)))

    def order(k):
        return z if k == 0 else NZ - 1 - z

    def block_sum_to(k, step, j):
        to = lax.rem(order(k) + 1 + j, NZ)
        to_z = to if k == 0 else NZ - 1 - to
        at = k * 3 + step
        return copy(bsum.at[at], binc.at[at], p2_s.at[at * 4 + j], p2_r.at[at], at_ctx(to_z, y))

    def gives(k, step):
        return lax.rem(order(k), 2 << step) == (1 << step) - 1

    def takes(k, step):
        return lax.rem(lax.div(order(k), 1 << step), 2) == 1

    def give(k, step):
        @pl.when(gives(k, step))
        def _():
            at = k * 3 + step
            bsum[at, :DH, :] = (jnp.exp(row_tot[...]) * before[...] + row_state[...]).astype(BF16)
            bsum[at, DH:, :] = coded(before_tot[...] + row_tot[...])
            for j in range(1 << step):
                block_sum_to(k, step, j).start()

    def take(k, step):
        @pl.when(takes(k, step))
        def _():
            at = k * 3 + step
            arrived(binc.at[at], p2_r.at[at], p2_s.at[at * 4])
            before[...] = jnp.exp(before_tot[...]) * binc[at, :DH, :].astype(F32) + before[...]
            before_tot[...] = before_tot[...] + decoded(binc[at, DH:, :])

    def carried_to_peer(k, j):
        at = k * 3 + j - 1
        return copy(cmsg.at[k, y_peer(j)], car.at[k, y], p3_s.at[at], p3_r.at[at], at_ctx(z, y_peer(j)))

    def send_states(k):
        st[k, y] = msg[k, y]
        for j in range(1, NY):
            state_to_peer(k, j).start()

    def join_row(k):
        for j in range(1, NY):
            at = k * 3 + j - 1
            arrived(st.at[k, y_from(j)], p1_r.at[at], p1_s.at[at])
        order = range(NY) if k == 0 else range(NY - 1, -1, -1)
        state = jnp.zeros((DH, DH), F32)
        so_far = jnp.zeros((1, DH), F32)
        for i in order:
            pre[i] = state
            lead_tot[i] = so_far
            tot = decoded(st[k, i, DH:, :])
            state = jnp.exp(tot) * state + st[k, i, :DH, :].astype(F32)
            so_far = so_far + tot
        row_state[...] = state
        row_tot[...] = so_far
        before[...] = jnp.zeros((DH, DH), F32)
        before_tot[...] = jnp.zeros((1, DH), F32)
        give(k, 0)

    def join_blocks(k, step):
        take(k, step)
        give(k, step + 1)

    def join_all(k):
        take(k, 2)
        for i in range(NY):
            cmsg[k, i] = (pre[i] + jnp.exp(lead_tot[i]) * before[...]).astype(BF16)
        car[k, y] = cmsg[k, y]
        for j in range(1, NY):
            carried_to_peer(k, j).start()

    def take_carried(k):
        for j in range(1, NY):
            at = k * 3 + j - 1
            arrived(car.at[k, y_from(j)], p3_r.at[at], p3_s.at[at])

    logs = jnp.concatenate([ld[...], jnp.zeros((8 - HEADS, TOK), F32)], axis=0)
    earlier = lax.broadcasted_iota(jnp.int32, (TOK, TOK), 0)
    later = lax.broadcasted_iota(jnp.int32, (TOK, TOK), 1)
    log_rows = nn(logs, (earlier <= later).astype(F32), EXACT)
    log_cols = nt((later <= earlier).astype(F32), logs, EXACT)
    causal = earlier >= later
    for h in range(HEADS):
        col = log_cols[:, h : h + 1]
        row = log_rows[h : h + 1, :]
        tot = log_rows[h : h + 1, TOK - 1 :]
        dec = jnp.exp(jnp.where(causal, col - row, NEG))
        decay[h] = dec
        tail = jnp.broadcast_to(jnp.exp(tot - col), (TOK, DH))
        tail_s[h] = tail
        lead_s[h] = jnp.broadcast_to(jnp.exp(col), (TOK, DH))
        kk = lk[:, cols(h)]
        weights[h] = (nt(lq[:, cols(h)], kk) * dec).astype(BF16)
        msg[0, h, :DH, :] = tn((kk.astype(F32) * tail).astype(BF16), lv[:, cols(h)]).astype(BF16)
        code = coded(jnp.broadcast_to(tot, (1, DH)))
        msg[0, h, DH:, :] = code
        msg[1, h, DH:, :] = code
    send_states(0)

    def gated(h):
        sig = jax.nn.sigmoid(gate[:, cols(h)].astype(F32))
        return sig, gain[:, cols(h)], lgrad[:, cols(h)].astype(F32)

    def sums_to(j):
        return copy(tps, tpr.at[j], tp_s.at[j - 1], tp_r.at[j - 1], {"tp": lax.rem(tp + j, NT)})

    def attend():
        take_carried(0)
        squares = jnp.zeros((TOK, DH), F32)
        cross = jnp.zeros((TOK, DH), F32)
        for h in range(HEADS):
            a = nn(weights[h], lv[:, cols(h)]) + lead_s[h] * nn(lq[:, cols(h)], car[0, h])
            att[:, cols(h)] = a
            sig, gn, gr = gated(h)
            squares = squares + a * a
            cross = cross + gr * gn * sig * a
        ones = jnp.ones((8, DH), F32)
        tps[0:8, :] = nt(ones, squares, EXACT)
        tps[8:16, :] = nt(ones, cross, EXACT)
        for j in range(1, NT):
            sums_to(j).start()

    def norm_and_grad():
        tot = tps[...]
        for j in range(1, NT):
            arrived(tpr.at[j], tp_r.at[j - 1], tp_s.at[j - 1])
            tot = tot + tpr[j]
        rms_row = lax.rsqrt(tot[0:8] / WIDTH + 1e-05)
        mean_row = rms_row * tot[8:16] / WIDTH
        eye = (earlier == later).astype(F32)
        rms = nt(eye, rms_row, EXACT)[:, 0:1]
        mean = nt(eye, mean_row, EXACT)[:, 0:1]
        for h in range(HEADS):
            sig, gn, gr = gated(h)
            normed = att[:, cols(h)] * rms
            by_gain = normed * gn * sig
            lin_out[:, cols(h)] = by_gain.astype(BF16)
            dgate[:, cols(h)] = (gr * by_gain * (1.0 - sig)).astype(BF16)
            da = (rms * (gr * gn * sig - normed * mean)).astype(BF16)
            gr_att[:, cols(h)] = da
            gweights[h] = (nt(da, lv[:, cols(h)]) * decay[h]).astype(BF16)
            msg[1, h, :DH, :] = tn((lq[:, cols(h)].astype(F32) * lead_s[h]).astype(BF16), da).astype(BF16)
        send_states(1)

    def lin_grads():
        take_carried(1)
        for h in range(HEADS):
            da = gr_att[:, cols(h)]
            kk = lk[:, cols(h)]
            dlq[:, cols(h)] = (nn(gweights[h], kk) + lead_s[h] * nt(da, car[0, h])).astype(BF16)
            dlk[:, cols(h)] = (
                tn(gweights[h], lq[:, cols(h)]) + tail_s[h] * nt(lv[:, cols(h)], car[1, h])
            ).astype(BF16)
            dlv[:, cols(h)] = (tn(weights[h], da) + tail_s[h] * nn(kk, car[1, h])).astype(BF16)

    def fwd_tile(h, keys, values_t, key_start):
        s = nn(keys, q_t[h])
        if key_start is not None:
            key_at = key_start + lax.broadcasted_iota(jnp.int32, s.shape, 0)
            query_at = y * TOK + lax.broadcasted_iota(jnp.int32, s.shape, 1)
            s = jnp.where(key_at <= query_at, s, NEG)
        old = peak[h]
        new = jnp.maximum(old, jnp.max(s, axis=0, keepdims=True))
        shrink = jnp.exp2((old - new) * EXP_SCALE)
        p = jnp.exp2((s - new) * EXP_SCALE)
        peak[h] = new
        total[h] = total[h] * shrink + jnp.sum(p, axis=0, keepdims=True)
        out_t[h] = out_t[h] * shrink + nn(values_t, p.astype(BF16))

    def fwd_row(d):
        rows = row_at(z - d)
        v_t[...] = vall[rows, :].T

        for h in range(HEADS):
            fwd_tile(h, kall[rows, :], v_t[...], None)

    def fwd_diagonal():
        for h in range(HEADS):
            peak[h] = jnp.full((1, TOK), NEG, F32)
            total[h] = jnp.zeros((1, TOK), F32)
            out_t[h] = jnp.zeros((DH, TOK), F32)

        rows = row_at(z)
        v_t[...] = vall[rows, :].T
        for h in range(HEADS):
            fwd_tile(h, kall[rows, :], v_t[...], 0)

    def finish_forward():
        for h in range(HEADS):
            o = (out_t[h] / total[h]).astype(BF16)
            sout[:, cols(h)] = o.T
            delta_s[h] = jnp.sum(g_t[h].astype(F32) * o.astype(F32), axis=0, keepdims=True)
            log_s[h] = peak[h] * EXP_SCALE + jnp.log(total[h]) * LOG2E
            dq_t[h] = jnp.zeros((DH, TOK), F32)

    def bwd_tile(h, keys, values, keys_t, key_start):
        s = nn(keys, q_t[h])
        p = jnp.exp2(s * EXP_SCALE - log_s[h])
        if key_start is not None:
            key_at = key_start + lax.broadcasted_iota(jnp.int32, s.shape, 0)
            query_at = y * TOK + lax.broadcasted_iota(jnp.int32, s.shape, 1)
            p = jnp.where(key_at <= query_at, p, 0.0)
        dp = nn(values, g_t[h])
        ds = (p * (dp - delta_s[h])).astype(BF16)
        dq_t[h] = dq_t[h] + nn(keys_t, ds)
        return nn(ds, sq[:, cols(h)]), nn(p.astype(BF16), so[:, cols(h)])

    def bwd_row(d, start=None):
        rows = row_at(z - d)
        k_t[...] = kall[rows, :].T

        for h in range(HEADS):
            dk, dv = bwd_tile(h, kall[rows, :], vall[rows, :], k_t[...], start)
            dk_acc[...] = dk if h == 0 else dk_acc[...] + dk
            dv_acc[...] = dv if h == 0 else dv_acc[...] + dv

    def local_block(yy):
        return pl.ds(pl.multiple_of(yy * TOK, TOK), TOK)

    def target(d, half=0):
        near = d <= 4 - half
        to_z = jnp.where(near, z - 1, jnp.where(up, z + 1, z - d))
        slot = jnp.where(near, d - 1, jnp.where(up, d + 1, 4))
        return to_z, slot

    def has_incoming(d, half=0):
        return ((d <= 3 - half) & up) | (d >= 6 - half)

    def half_row(half):
        return pl.ds(half * (ROW // 2), ROW // 2)

    def dk_copy(d, half):
        to_z, slot = target(d, half)
        src, dst = dks.at[d, half_row(half)], dkr.at[slot, half_row(half)]
        return copy(src, dst, dk_s.at[d * 2 + half], dk_r.at[slot * 2 + half], at_ctx(to_z, y))

    def add_dk(slot, half):
        at = slot * 2 + half
        rows = half_row(half)
        arrived(dkr.at[slot, rows], dk_r.at[at], dk_s.at[at])
        dk_acc[rows, :] = dk_acc[rows, :] + dkr[slot, rows, :].astype(F32)

    def dv_copy(d):
        to_z, slot = target(d)
        return copy(dvz.at[d], dvr.at[slot], dv_s.at[d], dv_r.at[slot], at_ctx(to_z, y))

    def dv_to_peer(d, j):
        at = d * 3 + j - 1
        src = dvs.at[d, local_block(y_peer(j))]
        return copy(src, dvy.at[d, j], dvy_s.at[at], dvy_r.at[at], at_ctx(z, y_peer(j)))

    def dk_to_peer(j):
        src = dks.at[0, local_block(y_peer(j))]
        return copy(src, dky.at[j], dky_s.at[j - 1], dky_r.at[j - 1], at_ctx(z, y_peer(j)))

    def spread_dv(d):
        dvs[d] = dv_acc[...].astype(BF16)
        dv_own[d] = dv_acc[local_block(y), :]
        for j in range(1, NY):
            dv_to_peer(d, j).start()

    def own_dv(d):
        acc = dv_own[d]
        for j in range(1, NY):
            at = d * 3 + j - 1
            arrived(dvy.at[d, j], dvy_r.at[at], dvy_s.at[at])
            acc = acc + dvy[d, j].astype(F32)
        return acc

    def add_incoming(acc, slots, sems, others, slot):
        arrived(slots.at[slot], sems.at[slot], others.at[slot])
        acc[...] = acc[...] + slots[slot].astype(F32)

    def pass_dk(d):
        for half in range(2):
            pl.when(has_incoming(d, half))(lambda: add_dk(d, half))
            rows = half_row(half)
            dks[d, rows, :] = dk_acc[rows, :].astype(BF16)
            dk_copy(d, half).start()

    part = dv_acc.at[pl.ds(0, TOK)]

    def pass_dv(d):
        @pl.when(z >= d)
        def _():
            part[...] = own_dv(d)

            @pl.when(has_incoming(d))
            def _():
                add_incoming(part, dvr, dv_r, dv_s, d)

            dvz[d] = part[...].astype(BF16)
            dv_copy(d).start()

    def bwd_order(t):
        return jnp.where(lax.rem(t, 2) == 0, 4 - lax.div(t, 2), 5 + lax.div(t - 1, 2))

    fetch_values(1)
    fetch_keys(1, 0)
    peer_values(0)
    fwd_diagonal()
    fetch_keys(1, 1)

    def at_steps(now, events):
        for at, event in events:
            pl.when(now == at)(event)

    def fwd_step(s, c):
        @pl.when(s < 4)
        def _():
            fetch_values(s + 1)
            fetch_keys(s + 1, 0)

        @pl.when(z >= s)
        def _():
            peer_values(s)
            fwd_row(s)

        at_steps(s, [(1, lambda: join_row(0))])

        @pl.when(s < 4)
        def _():
            fetch_keys(s + 1, 1)

            @pl.when(z + s >= NZ)
            def _():
                peer_values(NZ - s)
                fwd_row(NZ - s)

        at_steps(s, [(1, lambda: join_blocks(0, 0)), (2, lambda: join_blocks(0, 1)), (3, lambda: join_all(0)), (4, lambda: attend())])
        return c

    lax.fori_loop(1, 5, fwd_step, 0)
    finish_forward()

    def bwd_step(t, c):
        d = bwd_order(t)

        @pl.when(z >= d)
        def _():
            bwd_row(d)
            spread_dv(d)
            pass_dk(d)

        @pl.when(t > 0)
        def _():
            pass_dv(bwd_order(t - 1))

        at_steps(t, [(0, lambda: norm_and_grad()), (1, lambda: join_row(1)), (2, lambda: join_blocks(1, 0)), (3, lambda: join_blocks(1, 1)), (4, lambda: join_all(1)), (6, lambda: lin_grads())])
        return c

    lax.fori_loop(0, NZ - 1, bwd_step, 0)
    bwd_row(0, 0)
    spread_dv(0)

    @pl.when(up)
    def _():
        add_dk(0, 0)
        add_dk(0, 1)

    for half in range(2):
        pl.when(z <= 2 + half)(lambda: add_dk(4, half))

    dks[0] = dk_acc[...].astype(BF16)
    for j in range(1, NY):
        dk_to_peer(j).start()
    pass_dv(1)
    for h in range(HEADS):
        dsq[:, cols(h)] = (dq_t[h] * SCALE).T.astype(BF16)
    part[...] = own_dv(0)

    @pl.when(up)
    def _():
        add_incoming(part, dvr, dv_r, dv_s, 0)

    @pl.when(low)
    def _():
        add_incoming(part, dvr, dv_r, dv_s, 4)

    dsv[...] = part[...].astype(BF16)
    acc = dk_acc[local_block(y), :]
    for j in range(1, NY):
        arrived(dky.at[j], dky_r.at[j - 1], dky_s.at[j - 1])
        acc = acc + dky[j].astype(F32)
    dsk[...] = (acc * SCALE).astype(BF16)

    for j in range(1, NY):
        key_to_peer(j).wait_send()
        dk_to_peer(j).wait_send()
        for k in range(2):
            state_to_peer(k, j).wait_send()
            carried_to_peer(k, j).wait_send()
    for j in range(1, NT):
        sums_to(j).wait_send()
    for k in range(2):
        for step in range(3):

            @pl.when(gives(k, step))
            def _():
                for j in range(1 << step):
                    block_sum_to(k, step, j).wait_send()

    def passed_on(s, c):
        pl.when(z >= s)(lambda: upward(s, lambda *a: value_to(*a).wait_send(), True))
        pl.when((s < 3) & (rem_z(z + s) <= 2))(lambda: downward(s, lambda *a: value_to(*a).wait_send(), True))
        for half in range(2):
            gone = lambda *a: row_to(*a, half).wait_send()
            pl.when(z >= s)(lambda: upward(s, gone, s < 4 - half))
            pl.when(rem_z(z + s) <= 2 + half)(lambda: downward(s, gone, s < 3 + half))
        return c

    lax.fori_loop(0, 4, passed_on, 0)

    def all_gone(d, c):
        @pl.when(z >= d)
        def _():
            for j in range(1, NY):
                value_to_peer(d, j).wait_send()
                dv_to_peer(d, j).wait_send()

            @pl.when(d >= 1)
            def _():
                dk_copy(d, 0).wait_send()
                dk_copy(d, 1).wait_send()
                dv_copy(d).wait_send()

        return c

    lax.fori_loop(0, NZ, all_gone, 0)


def hand_over(*refs):
    for given, made in zip(refs[:9], refs[9:]):
        made[...] = given[...]


def body(lin_query, lin_key, lin_value, log_decay, norm_gain, lin_gate, lin_grad, soft_query, soft_key, soft_value, soft_grad):
    wide = jax.ShapeDtypeStruct((TOK, HEADS * DH), BF16)
    narrow = jax.ShapeDtypeStruct((TOK, DH), BF16)
    dma = pltpu.SemaphoreType.DMA
    vmem = pltpu.VMEM
    scratch = [
        vmem((NZ * ROW, DH), BF16),
        vmem((NZ * ROW, DH), BF16),
        vmem((HEADS, DH, TOK), BF16),
        vmem((HEADS, DH, TOK), BF16),
        vmem((DH, ROW), BF16),
        vmem((DH, ROW), BF16),
        vmem((HEADS, 1, TOK), F32),
        vmem((HEADS, 1, TOK), F32),
        vmem((HEADS, DH, TOK), F32),
        vmem((HEADS, 1, TOK), F32),
        vmem((HEADS, 1, TOK), F32),
        vmem((HEADS, DH, TOK), F32),
        vmem((ROW, DH), F32),
        vmem((ROW, DH), F32),
        vmem((NZ, ROW, DH), BF16),
        vmem((NZ, ROW, DH), BF16),
        vmem((NZ, ROW, DH), BF16),
        vmem((NZ, NY, TOK, DH), BF16),
        vmem((NZ, TOK, DH), F32),
        vmem((NZ, TOK, DH), BF16),
        vmem((NZ, TOK, DH), BF16),
        vmem((NY, TOK, DH), BF16),
        vmem((HEADS, TOK, TOK), F32),
        vmem((HEADS, TOK, TOK), BF16),
        vmem((HEADS, TOK, TOK), BF16),
        vmem((HEADS, TOK, DH), F32),
        vmem((HEADS, TOK, DH), F32),
        vmem((TOK, HEADS * DH), F32),
        vmem((TOK, HEADS * DH), BF16),
        vmem((2, HEADS, MSG, DH), BF16),
        vmem((2, NY, MSG, DH), BF16),
        vmem((NY, DH, DH), F32),
        vmem((NY, 1, DH), F32),
        vmem((DH, DH), F32),
        vmem((1, DH), F32),
        vmem((DH, DH), F32),
        vmem((1, DH), F32),
        vmem((6, MSG, DH), BF16),
        vmem((6, MSG, DH), BF16),
        vmem((2, NY, DH, DH), BF16),
        vmem((2, HEADS, DH, DH), BF16),
        vmem((16, TOK), F32),
        vmem((NT, 16, TOK), F32),
        dma((3,)), dma((3,)),
        dma((2 * NZ + 2,)), dma((2 * NZ + 2,)),
        dma((NZ,)), dma((NZ,)),
        dma((3 * NZ,)), dma((3 * NZ,)),
        dma((6,)), dma((6,)),
        dma((24,)), dma((6,)),
        dma((6,)), dma((6,)),
        dma((NT - 1,)), dma((NT - 1,)),
        dma((2 * NZ,)), dma((2 * NZ,)),
        dma((NZ,)), dma((NZ,)),
        dma((3 * NZ,)), dma((3 * NZ,)),
        dma((3,)), dma((3,)),
    ]
    shapes = [wide] * 7 + [narrow] * 2
    made = pl.pallas_call(
        kernel,
        out_shape=shapes,
        in_specs=[pl.BlockSpec(memory_space=pltpu.VMEM)] * 11,
        out_specs=[pl.BlockSpec(memory_space=pltpu.VMEM)] * 9,
        scratch_shapes=scratch,
        compiler_params=pltpu.CompilerParams(
            collective_id=0, has_side_effects=True, vmem_limit_bytes=56 * 2**20
        ),
    )(
        lin_query, lin_key, lin_value, log_decay, norm_gain.reshape(1, -1), lin_gate, lin_grad,
        soft_query, soft_key, soft_value, soft_grad,
    )
    whole = pl.BlockSpec(memory_space=pltpu.VMEM)
    return pl.pallas_call(
        hand_over,
        out_shape=shapes,
        in_specs=[whole] * 9,
        out_specs=[whole] * 9,
    )(*made)


def solution(mesh):
    shared = P("ctx", "tp")
    return jax.shard_map(
        lambda *args: tuple(body(*args)),
        mesh=mesh,
        in_specs=(shared, shared, shared, P("tp", "ctx"), P("tp"), shared, shared, shared, shared, shared, shared),
        out_specs=(shared,) * 9,
        check_vma=False,
    )
```

```python
import math

import jax
import jax.numpy as jnp
from jax import lax
from jax.experimental import pallas as pl
from jax.experimental.pallas import tpu as pltpu
from jax.sharding import PartitionSpec as P

DH = 128
HEADS = 4
TOK = 256
NY = 4
NZ = 8
NT = 8
ROW = NY * TOK
WIDTH = 4096
MSG = DH + 16
F32 = jnp.float32
BF16 = jnp.bfloat16
MESH = pl.DeviceIdType.MESH
SCALE = DH ** (-0.5)
LOG2E = math.log2(math.e)
EXP_SCALE = SCALE * LOG2E
NEG = -1e30
EXACT = lax.Precision.HIGHEST


def nn(a, b, precision=None):
    return lax.dot_general(a, b, (((1,), (0,)), ((), ())), precision=precision, preferred_element_type=F32)


def nt(a, b, precision=None):
    return lax.dot_general(a, b, (((1,), (1,)), ((), ())), precision=precision, preferred_element_type=F32)


def tn(a, b, precision=None):
    return lax.dot_general(a, b, (((0,), (0,)), ((), ())), precision=precision, preferred_element_type=F32)


def cols(h):
    return slice(h * DH, (h + 1) * DH)


def kernel(
    lq, lk, lv, ld, gain, gate, lgrad, sq, sk, sv, so,
    lin_out, dlq, dlk, dlv, dgate, sout, dsq, dsk, dsv,
    kall, vall, q_t, g_t, v_t, k_t, peak, total, out_t, log_s, delta_s, dq_t, dk_acc, dv_acc,
    dks, dkr, dvs, dvy, dv_own, dvz, dvr, dky,
    decay, weights, gweights, tail_s, lead_s, att, gr_att, msg, st, pre, lead_tot, row_state, row_tot, before, before_tot, bsum, binc, cmsg, car, tps, tpr,
    ky_s, ky_r, ks_s, kr_r, vs_s, vr_r, vy_s, vy_r, p1_s, p1_r, p2_s, p2_r, p3_s, p3_r, tp_s, tp_r,
    dk_s, dk_r, dv_s, dv_r, dvy_s, dvy_r, dky_s, dky_r,
):
    ctx = lax.axis_index("ctx")
    tp = lax.axis_index("tp")
    z = lax.div(ctx, NY)
    y = lax.rem(ctx, NY)

    def at_ctx(zz, yy):
        return {"ctx": zz * NY + yy}

    def y_peer(j):
        return lax.rem(y + j, NY)

    def y_from(j):
        return lax.rem(y + NY - j, NY)

    def copy(src, dst, s, r, device):
        return pltpu.make_async_remote_copy(
            src_ref=src, dst_ref=dst, send_sem=s, recv_sem=r, device_id=device, device_id_type=MESH
        )

    neighbour = at_ctx(z, y_peer(1))

    def arrived(dst, r, s):
        copy(dst, dst, s, r, neighbour).wait_recv()

    def sent(src, s, r):
        copy(src, src, s, r, neighbour).wait_send()

    barrier = pltpu.get_barrier_semaphore()
    for j in range(1, NY):
        pl.semaphore_signal(barrier, inc=1, device_id=at_ctx(z, y_peer(j)), device_id_type=MESH)
    for j in range(1, NZ):
        pl.semaphore_signal(barrier, inc=1, device_id=at_ctx(lax.rem(z + j, NZ), y), device_id_type=MESH)
    for j in range(1, NT):
        pl.semaphore_signal(barrier, inc=1, device_id={"tp": lax.rem(tp + j, NT)}, device_id_type=MESH)
    pl.semaphore_wait(barrier, NY + NZ + NT - 3)

    def block_at(zz, yy):
        return pl.ds(pl.multiple_of((zz * NY + yy) * TOK, TOK), TOK)

    def row_at(zz):
        return pl.ds(pl.multiple_of(zz * ROW, ROW), ROW)

    def key_to_peer(j):
        return copy(sk, kall.at[block_at(z, y)], ky_s.at[j - 1], ky_r.at[j - 1], at_ctx(z, y_peer(j)))

    def value_to_peer(d, j):
        ref = vall.at[block_at(z - d, y)]
        at = d * 3 + j - 1
        return copy(ref, ref, vy_s.at[at], vy_r.at[at], at_ctx(z, y_peer(j)))

    up = z < NZ - 1
    low = z <= 2

    def rem_z(zz):
        return lax.rem(zz + NZ, NZ)

    def half_of(zz, half):
        return pl.ds(pl.multiple_of(zz * ROW + half * (ROW // 2), ROW // 2), ROW // 2)

    def row_to(zz, to_z, step, half):
        ref = kall.at[half_of(zz, half)]
        at = step * 2 + half
        return copy(ref, ref, ks_s.at[at], kr_r.at[at], at_ctx(to_z, y))

    def value_to(zz, to_z, step):
        ref = vall.at[block_at(zz, y)]
        return copy(ref, ref, vs_s.at[step], vr_r.at[step], at_ctx(to_z, y))

    def upward(s, act, more):
        pl.when(up & more)(lambda: act(z - s, z + 1, s + 1))

    def downward(s, act, more):
        pl.when(more)(lambda: act(rem_z(z + s), rem_z(z - 1), s + 5))

    def fetch_values(s):
        @pl.when(z >= s)
        def _():
            arrived(vall.at[block_at(z - s, y)], vr_r.at[s], vs_s.at[s])
            upward(s, lambda *a: value_to(*a).start(), s < 4)
            for j in range(1, NY):
                value_to_peer(s, j).start()

        @pl.when((s <= 3) & (rem_z(z + s) <= 2))
        def _():
            arrived(vall.at[block_at(rem_z(z + s), y)], vr_r.at[s + 4], vs_s.at[s + 4])
            downward(s, lambda *a: value_to(*a).start(), s < 3)

            @pl.when(z + s >= NZ)
            def _():
                for j in range(1, NY):
                    value_to_peer(NZ - s, j).start()

    def fetch_keys(s, half):
        @pl.when((s <= 4 - half) & (z >= s))
        def _():
            at = s * 2 + half
            arrived(kall.at[half_of(z - s, half)], kr_r.at[at], ks_s.at[at])
            upward(s, lambda *a: row_to(*a, half).start(), s < 4 - half)

        @pl.when((s <= 3 + half) & (rem_z(z + s) <= 2 + half))
        def _():
            at = (s + 4) * 2 + half
            arrived(kall.at[half_of(rem_z(z + s), half)], kr_r.at[at], ks_s.at[at])
            downward(s, lambda *a: row_to(*a, half).start(), s < 3 + half)

    def peer_values(d):
        for j in range(1, NY):
            at = d * 3 + j - 1
            arrived(vall.at[block_at(z - d, y_from(j))], vy_r.at[at], vy_s.at[at])

    kall[block_at(z, y), :] = sk[...]
    vall[block_at(z, y), :] = sv[...]
    for j in range(1, NY):
        key_to_peer(j).start()

    upward(0, lambda *a: value_to(*a).start(), True)
    downward(0, lambda *a: value_to(*a).start(), low)
    for j in range(1, NY):
        value_to_peer(0, j).start()

    for h in range(HEADS):
        q_t[h] = sq[:, cols(h)].T
        g_t[h] = so[:, cols(h)].T

    for j in range(1, NY):
        arrived(kall.at[block_at(z, y_from(j))], ky_r.at[j - 1], ky_s.at[j - 1])

    for half in range(2):
        upward(0, lambda *a: row_to(*a, half).start(), True)
        downward(0, lambda *a: row_to(*a, half).start(), z <= 2 + half)

    def coded(tot):
        first = tot.astype(BF16).astype(F32)
        second = (tot - first).astype(BF16).astype(F32)
        third = (tot - first - second).astype(BF16).astype(F32)
        r = lax.broadcasted_iota(jnp.int32, (16, DH), 0)
        rows = jnp.where(r == 0, first, jnp.where(r == 1, second, jnp.where(r == 2, third, 0.0)))
        return rows.astype(BF16)

    def decoded(rows):
        return jnp.sum(rows.astype(F32), axis=0, keepdims=True)

    def state_to_peer(k, j):
        at = k * 3 + j - 1
        return copy(msg.at[k, y_peer(j)], st.at[k, y], p1_s.at[at], p1_r.at[at], at_ctx(z, y_peer(j)))

    def order(k):
        return z if k == 0 else NZ - 1 - z

    def block_sum_to(k, step, j):
        to = lax.rem(order(k) + 1 + j, NZ)
        to_z = to if k == 0 else NZ - 1 - to
        at = k * 3 + step
        return copy(bsum.at[at], binc.at[at], p2_s.at[at * 4 + j], p2_r.at[at], at_ctx(to_z, y))

    def gives(k, step):
        return lax.rem(order(k), 2 << step) == (1 << step) - 1

    def takes(k, step):
        return lax.rem(lax.div(order(k), 1 << step), 2) == 1

    def give(k, step):
        @pl.when(gives(k, step))
        def _():
            at = k * 3 + step
            bsum[at, :DH, :] = (jnp.exp(row_tot[...]) * before[...] + row_state[...]).astype(BF16)
            bsum[at, DH:, :] = coded(before_tot[...] + row_tot[...])
            for j in range(1 << step):
                block_sum_to(k, step, j).start()

    def take(k, step):
        @pl.when(takes(k, step))
        def _():
            at = k * 3 + step
            arrived(binc.at[at], p2_r.at[at], p2_s.at[at * 4])
            before[...] = jnp.exp(before_tot[...]) * binc[at, :DH, :].astype(F32) + before[...]
            before_tot[...] = before_tot[...] + decoded(binc[at, DH:, :])

    def carried_to_peer(k, j):
        at = k * 3 + j - 1
        return copy(cmsg.at[k, y_peer(j)], car.at[k, y], p3_s.at[at], p3_r.at[at], at_ctx(z, y_peer(j)))

    def send_states(k):
        st[k, y] = msg[k, y]
        for j in range(1, NY):
            state_to_peer(k, j).start()

    def join_row(k):
        for j in range(1, NY):
            at = k * 3 + j - 1
            arrived(st.at[k, y_from(j)], p1_r.at[at], p1_s.at[at])
        order = range(NY) if k == 0 else range(NY - 1, -1, -1)
        state = jnp.zeros((DH, DH), F32)
        so_far = jnp.zeros((1, DH), F32)
        for i in order:
            pre[i] = state
            lead_tot[i] = so_far
            tot = decoded(st[k, i, DH:, :])
            state = jnp.exp(tot) * state + st[k, i, :DH, :].astype(F32)
            so_far = so_far + tot
        row_state[...] = state
        row_tot[...] = so_far
        before[...] = jnp.zeros((DH, DH), F32)
        before_tot[...] = jnp.zeros((1, DH), F32)
        give(k, 0)

    def join_blocks(k, step):
        take(k, step)
        give(k, step + 1)

    def join_all(k):
        take(k, 2)
        for i in range(NY):
            cmsg[k, i] = (pre[i] + jnp.exp(lead_tot[i]) * before[...]).astype(BF16)
        car[k, y] = cmsg[k, y]
        for j in range(1, NY):
            carried_to_peer(k, j).start()

    def take_carried(k):
        for j in range(1, NY):
            at = k * 3 + j - 1
            arrived(car.at[k, y_from(j)], p3_r.at[at], p3_s.at[at])

    logs = jnp.concatenate([ld[...], jnp.zeros((8 - HEADS, TOK), F32)], axis=0)
    earlier = lax.broadcasted_iota(jnp.int32, (TOK, TOK), 0)
    later = lax.broadcasted_iota(jnp.int32, (TOK, TOK), 1)
    log_rows = nn(logs, (earlier <= later).astype(F32), EXACT)
    log_cols = nt((later <= earlier).astype(F32), logs, EXACT)
    causal = earlier >= later
    for h in range(HEADS):
        col = log_cols[:, h : h + 1]
        row = log_rows[h : h + 1, :]
        tot = log_rows[h : h + 1, TOK - 1 :]
        dec = jnp.exp(jnp.where(causal, col - row, NEG))
        decay[h] = dec
        tail = jnp.broadcast_to(jnp.exp(tot - col), (TOK, DH))
        tail_s[h] = tail
        lead_s[h] = jnp.broadcast_to(jnp.exp(col), (TOK, DH))
        kk = lk[:, cols(h)]
        weights[h] = (nt(lq[:, cols(h)], kk) * dec).astype(BF16)
        msg[0, h, :DH, :] = tn((kk.astype(F32) * tail).astype(BF16), lv[:, cols(h)]).astype(BF16)
        code = coded(jnp.broadcast_to(tot, (1, DH)))
        msg[0, h, DH:, :] = code
        msg[1, h, DH:, :] = code
    send_states(0)

    def gated(h):
        sig = jax.nn.sigmoid(gate[:, cols(h)].astype(F32))
        return sig, gain[:, cols(h)], lgrad[:, cols(h)].astype(F32)

    def sums_to(j):
        return copy(tps, tpr.at[j], tp_s.at[j - 1], tp_r.at[j - 1], {"tp": lax.rem(tp + j, NT)})

    def attend():
        take_carried(0)
        squares = jnp.zeros((TOK, DH), F32)
        cross = jnp.zeros((TOK, DH), F32)
        for h in range(HEADS):
            a = nn(weights[h], lv[:, cols(h)]) + lead_s[h] * nn(lq[:, cols(h)], car[0, h])
            att[:, cols(h)] = a
            sig, gn, gr = gated(h)
            squares = squares + a * a
            cross = cross + gr * gn * sig * a
        ones = jnp.ones((8, DH), F32)
        tps[0:8, :] = nt(ones, squares, EXACT)
        tps[8:16, :] = nt(ones, cross, EXACT)
        for j in range(1, NT):
            sums_to(j).start()

    def norm_and_grad():
        tot = tps[...]
        for j in range(1, NT):
            arrived(tpr.at[j], tp_r.at[j - 1], tp_s.at[j - 1])
            tot = tot + tpr[j]
        rms_row = lax.rsqrt(tot[0:8] / WIDTH + 1e-05)
        mean_row = rms_row * tot[8:16] / WIDTH
        eye = (earlier == later).astype(F32)
        rms = nt(eye, rms_row, EXACT)[:, 0:1]
        mean = nt(eye, mean_row, EXACT)[:, 0:1]
        for h in range(HEADS):
            sig, gn, gr = gated(h)
            normed = att[:, cols(h)] * rms
            by_gain = normed * gn * sig
            lin_out[:, cols(h)] = by_gain.astype(BF16)
            dgate[:, cols(h)] = (gr * by_gain * (1.0 - sig)).astype(BF16)
            da = (rms * (gr * gn * sig - normed * mean)).astype(BF16)
            gr_att[:, cols(h)] = da
            gweights[h] = (nt(da, lv[:, cols(h)]) * decay[h]).astype(BF16)
            msg[1, h, :DH, :] = tn((lq[:, cols(h)].astype(F32) * lead_s[h]).astype(BF16), da).astype(BF16)
        send_states(1)

    def lin_grads():
        take_carried(1)
        for h in range(HEADS):
            da = gr_att[:, cols(h)]
            kk = lk[:, cols(h)]
            dlq[:, cols(h)] = (nn(gweights[h], kk) + lead_s[h] * nt(da, car[0, h])).astype(BF16)
            dlk[:, cols(h)] = (
                tn(gweights[h], lq[:, cols(h)]) + tail_s[h] * nt(lv[:, cols(h)], car[1, h])
            ).astype(BF16)
            dlv[:, cols(h)] = (tn(weights[h], da) + tail_s[h] * nn(kk, car[1, h])).astype(BF16)

    def fwd_tile(h, keys, values_t, key_start):
        s = nn(keys, q_t[h])
        if key_start is not None:
            key_at = key_start + lax.broadcasted_iota(jnp.int32, s.shape, 0)
            query_at = y * TOK + lax.broadcasted_iota(jnp.int32, s.shape, 1)
            s = jnp.where(key_at <= query_at, s, NEG)
        old = peak[h]
        new = jnp.maximum(old, jnp.max(s, axis=0, keepdims=True))
        shrink = jnp.exp2((old - new) * EXP_SCALE)
        p = jnp.exp2((s - new) * EXP_SCALE)
        peak[h] = new
        total[h] = total[h] * shrink + jnp.sum(p, axis=0, keepdims=True)
        out_t[h] = out_t[h] * shrink + nn(values_t, p.astype(BF16))

    def fwd_row(d):
        rows = row_at(z - d)
        v_t[...] = vall[rows, :].T

        for h in range(HEADS):
            fwd_tile(h, kall[rows, :], v_t[...], None)

    def fwd_diagonal():
        for h in range(HEADS):
            peak[h] = jnp.full((1, TOK), NEG, F32)
            total[h] = jnp.zeros((1, TOK), F32)
            out_t[h] = jnp.zeros((DH, TOK), F32)

        rows = row_at(z)
        v_t[...] = vall[rows, :].T
        for h in range(HEADS):
            fwd_tile(h, kall[rows, :], v_t[...], 0)

    def finish_forward():
        for h in range(HEADS):
            o = (out_t[h] / total[h]).astype(BF16)
            sout[:, cols(h)] = o.T
            delta_s[h] = jnp.sum(g_t[h].astype(F32) * o.astype(F32), axis=0, keepdims=True)
            log_s[h] = peak[h] * EXP_SCALE + jnp.log(total[h]) * LOG2E
            dq_t[h] = jnp.zeros((DH, TOK), F32)

    def bwd_tile(h, keys, values, keys_t, key_start):
        s = nn(keys, q_t[h])
        p = jnp.exp2(s * EXP_SCALE - log_s[h])
        if key_start is not None:
            key_at = key_start + lax.broadcasted_iota(jnp.int32, s.shape, 0)
            query_at = y * TOK + lax.broadcasted_iota(jnp.int32, s.shape, 1)
            p = jnp.where(key_at <= query_at, p, 0.0)
        dp = nn(values, g_t[h])
        ds = (p * (dp - delta_s[h])).astype(BF16)
        dq_t[h] = dq_t[h] + nn(keys_t, ds)
        return nn(ds, sq[:, cols(h)]), nn(p.astype(BF16), so[:, cols(h)])

    def bwd_row(d, start=None):
        rows = row_at(z - d)
        k_t[...] = kall[rows, :].T

        for h in range(HEADS):
            dk, dv = bwd_tile(h, kall[rows, :], vall[rows, :], k_t[...], start)
            dk_acc[...] = dk if h == 0 else dk_acc[...] + dk
            dv_acc[...] = dv if h == 0 else dv_acc[...] + dv

    def local_block(yy):
        return pl.ds(pl.multiple_of(yy * TOK, TOK), TOK)

    def target(d, half=0):
        near = d <= 4 - half
        to_z = jnp.where(near, z - 1, jnp.where(up, z + 1, z - d))
        slot = jnp.where(near, d - 1, jnp.where(up, d + 1, 4))
        return to_z, slot

    def has_incoming(d, half=0):
        return ((d <= 3 - half) & up) | (d >= 6 - half)

    def half_row(half):
        return pl.ds(half * (ROW // 2), ROW // 2)

    def dk_copy(d, half):
        to_z, slot = target(d, half)
        src, dst = dks.at[d, half_row(half)], dkr.at[slot, half_row(half)]
        return copy(src, dst, dk_s.at[d * 2 + half], dk_r.at[slot * 2 + half], at_ctx(to_z, y))

    def add_dk(slot, half):
        at = slot * 2 + half
        rows = half_row(half)
        arrived(dkr.at[slot, rows], dk_r.at[at], dk_s.at[at])
        dk_acc[rows, :] = dk_acc[rows, :] + dkr[slot, rows, :].astype(F32)

    def dv_copy(d):
        to_z, slot = target(d)
        return copy(dvz.at[d], dvr.at[slot], dv_s.at[d], dv_r.at[slot], at_ctx(to_z, y))

    def dv_to_peer(d, j):
        at = d * 3 + j - 1
        src = dvs.at[d, local_block(y_peer(j))]
        return copy(src, dvy.at[d, j], dvy_s.at[at], dvy_r.at[at], at_ctx(z, y_peer(j)))

    def dk_to_peer(j):
        src = dks.at[0, local_block(y_peer(j))]
        return copy(src, dky.at[j], dky_s.at[j - 1], dky_r.at[j - 1], at_ctx(z, y_peer(j)))

    def spread_dv(d):
        dvs[d] = dv_acc[...].astype(BF16)
        dv_own[d] = dv_acc[local_block(y), :]
        for j in range(1, NY):
            dv_to_peer(d, j).start()

    def own_dv(d):
        acc = dv_own[d]
        for j in range(1, NY):
            at = d * 3 + j - 1
            arrived(dvy.at[d, j], dvy_r.at[at], dvy_s.at[at])
            acc = acc + dvy[d, j].astype(F32)
        return acc

    def add_incoming(acc, slots, sems, others, slot):
        arrived(slots.at[slot], sems.at[slot], others.at[slot])
        acc[...] = acc[...] + slots[slot].astype(F32)

    def pass_dk(d):
        for half in range(2):
            pl.when(has_incoming(d, half))(lambda: add_dk(d, half))
            rows = half_row(half)
            dks[d, rows, :] = dk_acc[rows, :].astype(BF16)
            dk_copy(d, half).start()

    part = dv_acc.at[pl.ds(0, TOK)]

    def pass_dv(d):
        @pl.when(z >= d)
        def _():
            part[...] = own_dv(d)

            @pl.when(has_incoming(d))
            def _():
                add_incoming(part, dvr, dv_r, dv_s, d)

            dvz[d] = part[...].astype(BF16)
            dv_copy(d).start()

    def bwd_order(t):
        return jnp.where(lax.rem(t, 2) == 0, 4 - lax.div(t, 2), 5 + lax.div(t - 1, 2))

    fetch_values(1)
    fetch_keys(1, 0)
    peer_values(0)
    fwd_diagonal()
    fetch_keys(1, 1)

    def at_steps(now, events):
        for at, event in events:
            pl.when(now == at)(event)

    def fwd_step(s, c):
        @pl.when(s < 3)
        def _():
            fetch_values(s + 1)
            fetch_keys(s + 1, 0)

        @pl.when(s == 4)
        def _():
            fetch_keys(4, 0)
            fetch_keys(4, 1)

        @pl.when(z >= s)
        def _():
            peer_values(s)
            fwd_row(s)

        at_steps(s, [(1, lambda: join_row(0))])

        pl.when(s < 3)(lambda: fetch_keys(s + 1, 1))
        pl.when(s == 3)(lambda: fetch_values(4))

        @pl.when(s < 4)
        def _():

            @pl.when(z + s >= NZ)
            def _():
                peer_values(NZ - s)
                fwd_row(NZ - s)

        at_steps(s, [(1, lambda: join_blocks(0, 0)), (2, lambda: join_blocks(0, 1)), (3, lambda: join_all(0)), (4, lambda: attend())])
        return c

    lax.fori_loop(1, 5, fwd_step, 0)
    finish_forward()

    def bwd_step(t, c):
        d = bwd_order(t)

        @pl.when(z >= d)
        def _():
            bwd_row(d)
            spread_dv(d)
            pass_dk(d)

        @pl.when(t > 0)
        def _():
            pass_dv(bwd_order(t - 1))

        at_steps(t, [(0, lambda: norm_and_grad()), (1, lambda: join_row(1)), (2, lambda: join_blocks(1, 0)), (3, lambda: join_blocks(1, 1)), (4, lambda: join_all(1)), (6, lambda: lin_grads())])
        return c

    lax.fori_loop(0, NZ - 1, bwd_step, 0)
    bwd_row(0, 0)
    spread_dv(0)

    @pl.when(up)
    def _():
        add_dk(0, 0)
        add_dk(0, 1)

    for half in range(2):
        pl.when(z <= 2 + half)(lambda: add_dk(4, half))

    dks[0] = dk_acc[...].astype(BF16)
    for j in range(1, NY):
        dk_to_peer(j).start()
    pass_dv(1)
    for h in range(HEADS):
        dsq[:, cols(h)] = (dq_t[h] * SCALE).T.astype(BF16)
    part[...] = own_dv(0)

    @pl.when(up)
    def _():
        add_incoming(part, dvr, dv_r, dv_s, 0)

    @pl.when(low)
    def _():
        add_incoming(part, dvr, dv_r, dv_s, 4)

    dsv[...] = part[...].astype(BF16)
    acc = dk_acc[local_block(y), :]
    for j in range(1, NY):
        arrived(dky.at[j], dky_r.at[j - 1], dky_s.at[j - 1])
        acc = acc + dky[j].astype(F32)
    dsk[...] = (acc * SCALE).astype(BF16)

    for j in range(1, NY):
        key_to_peer(j).wait_send()
        dk_to_peer(j).wait_send()
        for k in range(2):
            state_to_peer(k, j).wait_send()
            carried_to_peer(k, j).wait_send()
    for j in range(1, NT):
        sums_to(j).wait_send()
    for k in range(2):
        for step in range(3):

            @pl.when(gives(k, step))
            def _():
                for j in range(1 << step):
                    block_sum_to(k, step, j).wait_send()

    def passed_on(s, c):
        pl.when(z >= s)(lambda: upward(s, lambda *a: value_to(*a).wait_send(), True))
        pl.when((s < 3) & (rem_z(z + s) <= 2))(lambda: downward(s, lambda *a: value_to(*a).wait_send(), True))
        for half in range(2):
            gone = lambda *a: row_to(*a, half).wait_send()
            pl.when(z >= s)(lambda: upward(s, gone, s < 4 - half))
            pl.when(rem_z(z + s) <= 2 + half)(lambda: downward(s, gone, s < 3 + half))
        return c

    lax.fori_loop(0, 4, passed_on, 0)

    def all_gone(d, c):
        @pl.when(z >= d)
        def _():
            for j in range(1, NY):
                value_to_peer(d, j).wait_send()
                dv_to_peer(d, j).wait_send()

            @pl.when(d >= 1)
            def _():
                dk_copy(d, 0).wait_send()
                dk_copy(d, 1).wait_send()
                dv_copy(d).wait_send()

        return c

    lax.fori_loop(0, NZ, all_gone, 0)


def hand_over(*refs):
    for given, made in zip(refs[:9], refs[9:]):
        made[...] = given[...]


def body(lin_query, lin_key, lin_value, log_decay, norm_gain, lin_gate, lin_grad, soft_query, soft_key, soft_value, soft_grad):
    wide = jax.ShapeDtypeStruct((TOK, HEADS * DH), BF16)
    narrow = jax.ShapeDtypeStruct((TOK, DH), BF16)
    dma = pltpu.SemaphoreType.DMA
    vmem = pltpu.VMEM
    scratch = [
        vmem((NZ * ROW, DH), BF16),
        vmem((NZ * ROW, DH), BF16),
        vmem((HEADS, DH, TOK), BF16),
        vmem((HEADS, DH, TOK), BF16),
        vmem((DH, ROW), BF16),
        vmem((DH, ROW), BF16),
        vmem((HEADS, 1, TOK), F32),
        vmem((HEADS, 1, TOK), F32),
        vmem((HEADS, DH, TOK), F32),
        vmem((HEADS, 1, TOK), F32),
        vmem((HEADS, 1, TOK), F32),
        vmem((HEADS, DH, TOK), F32),
        vmem((ROW, DH), F32),
        vmem((ROW, DH), F32),
        vmem((NZ, ROW, DH), BF16),
        vmem((NZ, ROW, DH), BF16),
        vmem((NZ, ROW, DH), BF16),
        vmem((NZ, NY, TOK, DH), BF16),
        vmem((NZ, TOK, DH), F32),
        vmem((NZ, TOK, DH), BF16),
        vmem((NZ, TOK, DH), BF16),
        vmem((NY, TOK, DH), BF16),
        vmem((HEADS, TOK, TOK), F32),
        vmem((HEADS, TOK, TOK), BF16),
        vmem((HEADS, TOK, TOK), BF16),
        vmem((HEADS, TOK, DH), F32),
        vmem((HEADS, TOK, DH), F32),
        vmem((TOK, HEADS * DH), F32),
        vmem((TOK, HEADS * DH), BF16),
        vmem((2, HEADS, MSG, DH), BF16),
        vmem((2, NY, MSG, DH), BF16),
        vmem((NY, DH, DH), F32),
        vmem((NY, 1, DH), F32),
        vmem((DH, DH), F32),
        vmem((1, DH), F32),
        vmem((DH, DH), F32),
        vmem((1, DH), F32),
        vmem((6, MSG, DH), BF16),
        vmem((6, MSG, DH), BF16),
        vmem((2, NY, DH, DH), BF16),
        vmem((2, HEADS, DH, DH), BF16),
        vmem((16, TOK), F32),
        vmem((NT, 16, TOK), F32),
        dma((3,)), dma((3,)),
        dma((2 * NZ + 2,)), dma((2 * NZ + 2,)),
        dma((NZ,)), dma((NZ,)),
        dma((3 * NZ,)), dma((3 * NZ,)),
        dma((6,)), dma((6,)),
        dma((24,)), dma((6,)),
        dma((6,)), dma((6,)),
        dma((NT - 1,)), dma((NT - 1,)),
        dma((2 * NZ,)), dma((2 * NZ,)),
        dma((NZ,)), dma((NZ,)),
        dma((3 * NZ,)), dma((3 * NZ,)),
        dma((3,)), dma((3,)),
    ]
    shapes = [wide] * 7 + [narrow] * 2
    made = pl.pallas_call(
        kernel,
        out_shape=shapes,
        in_specs=[pl.BlockSpec(memory_space=pltpu.VMEM)] * 11,
        out_specs=[pl.BlockSpec(memory_space=pltpu.VMEM)] * 9,
        scratch_shapes=scratch,
        compiler_params=pltpu.CompilerParams(
            collective_id=0, has_side_effects=True, vmem_limit_bytes=56 * 2**20
        ),
    )(
        lin_query, lin_key, lin_value, log_decay, norm_gain.reshape(1, -1), lin_gate, lin_grad,
        soft_query, soft_key, soft_value, soft_grad,
    )
    whole = pl.BlockSpec(memory_space=pltpu.VMEM)
    return pl.pallas_call(
        hand_over,
        out_shape=shapes,
        in_specs=[whole] * 9,
        out_specs=[whole] * 9,
    )(*made)


def solution(mesh):
    shared = P("ctx", "tp")
    return jax.shard_map(
        lambda *args: tuple(body(*args)),
        mesh=mesh,
        in_specs=(shared, shared, shared, P("tp", "ctx"), P("tp"), shared, shared, shared, shared, shared, shared),
        out_specs=(shared,) * 9,
        check_vma=False,
    )
```
